512 devices in a mesh: pts: 128 (over y, z, core), grp: 4 (over x).
Axes of the slice: x: 4, y: 4, z: 16, core: 2. Of those that a mesh axis runs over, the one named last changes fastest.
Arguments:
- features: bfloat16 [4, 65536, 256], P('grp', 'pts'), may hold values from -6 to 6
- hilbert_slot: int32 [4, 65536], P('grp', 'pts'), may hold values from 0 to 524287, as said below
- hilbert_count: int32 [4, 128], P('grp', 'pts'), may hold values from 256 to 1024, as said below
- norm_gain: float32 [2, 2, 256], replicated, may hold values from 0.1 to 1.9
- norm_shift: float32 [2, 2, 256], replicated, may hold values from -3 to 3
- qkv_weight: bfloat16 [2, 256, 768], replicated, may hold values from -0.75 to 0.75
- proj_weight: bfloat16 [2, 256, 256], replicated, may hold values from -0.375 to 0.375
- up_weight: bfloat16 [2, 256, 1024], replicated, may hold values from -0.375 to 0.375
- up_bias: float32 [2, 1024], replicated, may hold values from -3 to 3
- down_weight: bfloat16 [2, 1024, 256], replicated, may hold values from -0.1875 to 0.1875
- out_bias: float32 [2, 2, 256], replicated, may hold values from -3 to 3
Outputs:
- refined: bfloat16 [4, 65536, 256], P('grp', 'pts')
The draws below stay inside these ranges and needn't reach their ends.
Inputs may be any that keep to these rules, and one draw needn't show every extreme that they name: hilbert_slot = (owner group * 128 + owner index) * 1024 + position; every slot is used at most once and each owner's used positions are exactly those below its hilbert_count. The owner's group is the point's own, except that positions below 64 of index 0 of every group hold points of the previous group (the last group's go to group 0). Counting points for index 0 of the own group together with those that go on to the next group, no device sends more than 16 points to one index of its group, and some device sends exactly 16; every device sends exactly 16 points to each aligned four indices of its group. The last owner of the last group holds 1024 points. `hilbert_count`: in each aligned four owners of a group, one holds 1024 points and the four hold 2048 together.
All inputs are finite; a program needn't handle non-finite values.
Results may differ from the reference program's by a relative error of at most 0.034.
Values may be sent and summed in bfloat16 or wider, within the bound.
A program may use at most 64 MiB of HBM per device.

```python
import jax
import jax.numpy as jnp
from jax import lax

D = 256
HEADS = 16
FF = 1024
PATCH = 1024
BOUND = 64
ROWS = 512
OWNERS = 128
GROUPS = 4
SHARE = 16


def hilbert_layout(key):
    quad_count = OWNERS // 4
    pair_count = OWNERS // 2
    pair_cap = SHARE
    subkeys = jax.random.split(jax.random.fold_in(key, 11), 6)
    full_at = jax.random.randint(subkeys[0], (GROUPS, quad_count), 0, 4, dtype=jnp.int32)
    full_at = full_at.at[GROUPS - 1, quad_count - 1].set(3)
    lead_part = jax.random.randint(subkeys[1], (GROUPS, quad_count, pair_count), 0, pair_cap + 1, dtype=jnp.int32)
    chosen = jax.random.randint(subkeys[2], (GROUPS, quad_count), 0, pair_count, dtype=jnp.int32)
    pair_range = jnp.arange(pair_count, dtype=jnp.int32)
    lead_part = jnp.where(pair_range[None, None, :] == chosen[:, :, None], pair_cap, lead_part)
    extra_one = jax.random.randint(subkeys[3], (GROUPS, quad_count, pair_count), 0, pair_cap // 8 + 1, dtype=jnp.int32)
    extra_two = jax.random.randint(subkeys[4], (GROUPS, quad_count, pair_count), 0, pair_cap // 8 + 1, dtype=jnp.int32)
    part_one = pair_cap // 4 + extra_one
    part_two = pair_cap // 4 + extra_two
    part_three = pair_cap - part_one - part_two
    start_one = jnp.cumsum(part_one, axis=2) - part_one
    start_two = jnp.cumsum(part_two, axis=2) - part_two
    start_three = jnp.cumsum(part_three, axis=2) - part_three
    perm_keys = jax.random.split(subkeys[5], GROUPS * OWNERS)
    shuffle = jax.vmap(lambda single: jax.random.permutation(single, ROWS))(perm_keys)
    shuffle = shuffle.reshape(GROUPS, OWNERS, ROWS).astype(jnp.int32)
    quad_id = shuffle // pair_cap
    within = shuffle % pair_cap
    sender = jnp.arange(OWNERS, dtype=jnp.int32)[None, :, None]
    pair_id = sender % pair_count
    leading = sender < pair_count
    group_ids = jnp.arange(GROUPS, dtype=jnp.int32)[:, None, None]
    lead_row = lead_part[group_ids, quad_id, pair_id]
    to_full = jnp.where(leading, within < lead_row, within < pair_cap - lead_row)
    full_slot = pair_id * pair_cap + jnp.where(leading, within, lead_row + within)
    rest_index = jnp.where(leading, within - lead_row, within)
    size_one = part_one[group_ids, quad_id, pair_id]
    size_two = part_two[group_ids, quad_id, pair_id]
    rest_part = jnp.where(rest_index < size_one, 0, jnp.where(rest_index < size_one + size_two, 1, 2))
    rest_slot = jnp.where(rest_part == 0, start_one[group_ids, quad_id, pair_id] + rest_index, jnp.where(rest_part == 1, start_two[group_ids, quad_id, pair_id] + rest_index - size_one, start_three[group_ids, quad_id, pair_id] + rest_index - size_one - size_two))
    full_row = full_at[group_ids, quad_id]
    rest_place = rest_part + (rest_part >= full_row).astype(jnp.int32)
    owner_id = quad_id * 4 + jnp.where(to_full, full_row, rest_place)
    position = jnp.where(to_full, full_slot, rest_slot)
    crossing = (owner_id == 0) & (position < BOUND)
    target_group = jnp.where(crossing, (group_ids + 1) % GROUPS, group_ids)
    slot_ids = (target_group * OWNERS + owner_id) * PATCH + position
    totals = jnp.stack([part_one.sum(axis=2), part_two.sum(axis=2), part_three.sum(axis=2)], axis=2)
    column = jnp.arange(4, dtype=jnp.int32)[None, None, :]
    take_index = jnp.clip(column - (column > full_at[:, :, None]).astype(jnp.int32), 0, 2)
    rest_count = jnp.take_along_axis(totals, take_index, axis=2)
    counts = jnp.where(column == full_at[:, :, None], PATCH, rest_count).reshape(GROUPS, OWNERS)
    return (slot_ids.reshape(GROUPS, OWNERS * ROWS).astype(jnp.int32), counts.astype(jnp.int32))


def draw_hilbert_slot(key, part):
    layout = hilbert_layout(key)
    return layout[0]


def draw_hilbert_count(key, part):
    layout = hilbert_layout(key)
    return layout[1]


def block_levels(stream_key, extent, cuts, low, largest):
    def one(dim, parts):
        heights = jax.random.uniform(jax.random.fold_in(jax.random.fold_in(stream_key, 6), dim), (parts,), jnp.float32, low / len(cuts), largest / len(cuts))
        return jnp.repeat(jnp.exp(heights), extent[dim] // parts).reshape((-1,) + (1,) * (len(extent) - dim - 1))

    level = one(*cuts[0])
    for cut in cuts[1:]:
        level = level * one(*cut)
    return level


def normal_values(rng, dims, width, reach, cuts=(), held_as=jnp.bfloat16):
    level = block_levels(rng, dims, cuts, -0.22, 0.18) if cuts else 1.0
    array = jax.random.normal(rng, dims, jnp.float32) * width * level
    return jnp.minimum(jnp.maximum(array, -reach), reach).astype(held_as)


def setup_inputs(seed: int = 0) -> dict:
    streams_of = jax.random.split(jax.random.key(seed), 12)
    features = normal_values(streams_of[0], (GROUPS, OWNERS * ROWS, D), 1.0, 6.0, ((0, 4), (1, 128)))
    hilbert_slot = draw_hilbert_slot(jax.random.fold_in(streams_of[11], 71), 0)
    hilbert_count = draw_hilbert_count(jax.random.fold_in(streams_of[11], 71), 0)
    norm_gain = jnp.clip(1.0 + 0.18 * jax.random.normal(streams_of[3], (2, 2, D), jnp.float32), 0.1, 1.9)
    norm_shift = normal_values(streams_of[4], (2, 2, D), 0.3, 3.0, (), jnp.float32)
    qkv_weight = normal_values(streams_of[5], (2, D, 3 * D), (D // 4) ** -0.5, 0.75)
    proj_weight = normal_values(streams_of[6], (2, D, D), D ** -0.5, 0.375)
    up_weight = normal_values(streams_of[7], (2, D, FF), D ** -0.5, 0.375)
    up_bias = normal_values(streams_of[8], (2, FF), 0.3, 3.0, (), jnp.float32)
    down_weight = normal_values(streams_of[9], (2, FF, D), FF ** -0.5, 0.1875)
    out_bias = normal_values(streams_of[10], (2, 2, D), 0.3, 3.0, (), jnp.float32)
    return dict(features=features, hilbert_slot=hilbert_slot, hilbert_count=hilbert_count, norm_gain=norm_gain, norm_shift=norm_shift, qkv_weight=qkv_weight, proj_weight=proj_weight, up_weight=up_weight, up_bias=up_bias, down_weight=down_weight, out_bias=out_bias)


NORM_EPS = 1e-05

def layer_norm(input_rows, norm_scale, norm_offset):
    input_rows = input_rows.astype(jnp.float32)
    center = lax.optimization_barrier(jnp.mean(input_rows, axis=-1, keepdims=True))
    centered = input_rows - center
    spread = lax.optimization_barrier(jnp.mean(centered * centered, axis=-1, keepdims=True))
    return centered * lax.rsqrt(spread + NORM_EPS) * norm_scale + norm_offset

def patch_attention(normed, qkv_matrix, live_mask):
    qkv_rows = jnp.dot(normed, qkv_matrix, preferred_element_type=jnp.float32).astype(jnp.bfloat16)
    qkv_rows = lax.optimization_barrier(qkv_rows).astype(jnp.float32)
    point_count = normed.shape[0]
    head_dim = D // HEADS
    split_heads = qkv_rows.reshape(point_count, 3, HEADS, head_dim)
    queries = split_heads[:, 0]
    keys_all = split_heads[:, 1]
    values_all = split_heads[:, 2]
    scores = jnp.einsum('qhd,khd->hqk', queries, keys_all) * head_dim ** (-0.5)
    exp_scores = jnp.where(live_mask[None, None, :], jnp.exp(scores), 0.0)
    denominator = lax.optimization_barrier(jnp.sum(exp_scores, axis=2))
    weights_low = lax.optimization_barrier(exp_scores.astype(jnp.bfloat16)).astype(jnp.float32)
    attended = jnp.einsum('hqk,khd->qhd', weights_low, values_all) / jnp.transpose(denominator)[:, :, None]
    return attended.reshape(point_count, D).astype(jnp.bfloat16)

def attention_half(input_rows, live_mask, block, norm_gain, norm_shift, qkv_weight, proj_weight, out_bias):
    normed = layer_norm(input_rows, norm_gain[block, 0], norm_shift[block, 0]).astype(jnp.bfloat16)
    attended = patch_attention(normed, qkv_weight[block], live_mask)
    projected_out = jnp.dot(attended, proj_weight[block], preferred_element_type=jnp.float32) + out_bias[block, 0]
    return (input_rows.astype(jnp.float32) + projected_out).astype(jnp.bfloat16)

def feed_forward(input_rows, block, norm_gain, norm_shift, up_weight, up_bias, down_weight, out_bias):
    normed = layer_norm(input_rows, norm_gain[block, 1], norm_shift[block, 1]).astype(jnp.bfloat16)
    pre_act = jnp.dot(normed, up_weight[block], preferred_element_type=jnp.float32) + up_bias[block]
    hidden = jax.nn.gelu(pre_act, approximate=False).astype(jnp.bfloat16)
    projected_out = jnp.dot(hidden, down_weight[block], preferred_element_type=jnp.float32) + out_bias[block, 1]
    return (input_rows.astype(jnp.float32) + projected_out).astype(jnp.bfloat16)

def reference(features, hilbert_slot, hilbert_count, norm_gain, norm_shift, qkv_weight, proj_weight, up_weight, up_bias, down_weight, out_bias):
    total_rows = GROUPS * OWNERS * ROWS
    patched = features.reshape(total_rows // PATCH, PATCH, D)
    all_live = jnp.ones((PATCH,), jnp.bool_)

    def first_block(pieces):
        mixed_rows = attention_half(pieces, all_live, 0, norm_gain, norm_shift, qkv_weight, proj_weight, out_bias)
        return feed_forward(mixed_rows, 0, norm_gain, norm_shift, up_weight, up_bias, down_weight, out_bias)
    after_one = lax.map(first_block, patched).reshape(total_rows, D)
    slot_ids = hilbert_slot.reshape(total_rows).astype(jnp.int32)
    owner_rows = jnp.zeros((GROUPS * OWNERS * PATCH, D), after_one.dtype).at[slot_ids].set(after_one)
    owner_rows = owner_rows.reshape(GROUPS * OWNERS, PATCH, D)
    live_counts = hilbert_count.reshape(GROUPS * OWNERS)

    def second_half(pieces):
        patch_rows, live_count = pieces
        live_mask = jnp.arange(PATCH, dtype=jnp.int32) < live_count
        return attention_half(patch_rows, live_mask, 1, norm_gain, norm_shift, qkv_weight, proj_weight, out_bias)
    mixed_two = lax.map(second_half, (owner_rows, live_counts)).reshape(GROUPS * OWNERS * PATCH, D)
    returned = mixed_two[slot_ids].reshape(total_rows // PATCH, PATCH, D)

    def second_ff(pieces):
        return feed_forward(pieces, 1, norm_gain, norm_shift, up_weight, up_bias, down_weight, out_bias)
    refined = lax.map(second_ff, returned)
    return refined.reshape(GROUPS, OWNERS * ROWS, D)
```

```python
import functools

import jax
import jax.numpy as jnp
from jax import lax
from jax.experimental import pallas as pl
from jax.experimental.pallas import tpu as pltpu
from jax.sharding import PartitionSpec as P

BF = jnp.bfloat16
F32 = jnp.float32
I32 = jnp.int32
MESH = pl.DeviceIdType.MESH
NORM_EPS = 1e-05
SCALE = 0.25 * 1.4426950408889634
ROWS = 512
WIDTH = 256
PATCH = 1024
CROSS = 64
PEERS = 48


def layer_norm(rows, gain, shift):
    rows = rows.astype(F32)
    centered = rows - jnp.mean(rows, axis=-1, keepdims=True)
    spread = jnp.mean(centered * centered, axis=-1, keepdims=True)
    return (centered * lax.rsqrt(spread + NORM_EPS) * gain + shift).astype(BF)


def mm(left, right):
    return jnp.dot(left, right, preferred_element_type=F32)


def mm_nt(left, right):
    return lax.dot_general(left, right, (((1,), (1,)), ((), ())), preferred_element_type=F32)


def iota(shape, dim):
    return lax.broadcasted_iota(I32, shape, dim)


def onehot(mask):
    return jnp.where(mask, 1.0, 0.0).astype(BF)


def gelu(values):
    return 0.5 * values * (1.0 + lax.erf(values * 0.7071067811865476))


def pipelined(parts, score, finish):
    scores = score(parts[0])
    for index, part in enumerate(parts):
        ahead = score(parts[index + 1]) if index + 1 < len(parts) else None
        finish(part, scores)
        scores = ahead


def kernel(
    x_ref,
    slot_ref,
    gain_ref,
    shift_ref,
    qkv_ref,
    proj_ref,
    up_ref,
    upb_ref,
    down_ref,
    outb_ref,
    out_ref,
    px,
    xp,
    qbuf,
    kbuf,
    vobuf,
    send_a,
    recv_a,
    tag_send,
    tag_recv,
    tag_quad,
    zrows,
    gath,
    dsend,
    sort_m,
    unsort_m,
    home_m,
    gs,
    kpack,
    cross_out,
    cross_in,
    att_s,
    catt_out,
    catt_in,
    zatt_out,
    zatt_in,
    own_att,
    datt_out,
    datt_in,
    ret_send,
    home,
    ab_send,
    ab_recv,
    tag_ssem,
    tag_rsem,
    quad_ssem,
    quad_rsem,
    pair_sem,
    z_ssem,
    z_rsem,
    d_ssem,
    d_rsem,
    cross_sem,
    catt_sem,
    za_ssem,
    za_rsem,
    da_ssem,
    da_rsem,
    rt_ssem,
    rt_rsem,
):
    me = lax.axis_index("pts")
    grp = lax.axis_index("grp")
    core = me % 2
    half = (me // 2) % 2
    quad_z = (me // 4) % 8
    quad_y = me // 32
    base = me // 4 * 4
    other_core = base + half * 2 + (1 - core)
    other_chip = base + (1 - half) * 2 + core
    diagonal = base + (1 - half) * 2 + (1 - core)
    next_grp = (grp + 1) % 4
    last_grp = (grp + 3) % 4

    def place(dy, dz, chip_half):
        return (((quad_y + dy + 4) % 4) * 8 + (quad_z + dz + 8) % 8) * 4 + chip_half * 2 + core

    def copy_to(src, dst, ssem, rsem, pts=None, group=None):
        target = {"pts": pts} if group is None else {"grp": group}
        return pltpu.make_async_remote_copy(
            src_ref=src,
            dst_ref=dst,
            send_sem=ssem,
            recv_sem=rsem,
            device_id=target,
            device_id_type=MESH,
        )

    barrier = pltpu.get_barrier_semaphore()

    def greet(target):
        pl.semaphore_signal(barrier, inc=1, device_id=target, device_id_type=MESH)

    for dy in range(4):
        for dz in range(1, 4):
            greet({"pts": place(dy, dz, 0)})
            greet({"pts": place(dy, 8 - dz, 1)})
            greet({"pts": place(dy, (8 - dz) * (1 - half) + dz * half, half)})
        greet({"pts": place(dy, 4, 1 - half)})
        if dy:
            greet({"pts": place(dy, 0, half)})
    greet({"pts": other_core})
    greet({"pts": other_chip})
    greet({"pts": diagonal})
    greet({"grp": next_grp})
    greet({"grp": last_grp})

    slot = slot_ref[...]
    owner = slot // PATCH
    position = slot % PATCH
    index = jnp.where(owner // 128 == grp, owner % 128, 0)
    quad = index // 4
    dy_of = (quad // 8 - quad_y + 4) % 4
    dz_of = (quad % 8 - quad_z + 8) % 8
    turn = dz_of - 4
    place_of = 2 * jnp.abs(turn) - (turn < 0).astype(I32)
    block_of = place_of * 4 + dy_of
    inner = jnp.where(place_of % 2 == 1, place_of + half, place_of - 1 + half)
    kord_of = jnp.where(place_of == 0, 0, jnp.where(place_of == 7, 7, inner))
    in_block = onehot(iota((32, ROWS), 0) == block_of)
    upto = onehot(iota((ROWS, ROWS), 0) <= iota((ROWS, ROWS), 1))
    counted = mm(in_block, upto)
    rank = jnp.sum(in_block.astype(F32) * counted, axis=0, keepdims=True).astype(I32) - 1
    row_of = block_of * 16 + rank
    perm = onehot(iota((ROWS, ROWS), 0) == row_of)
    rows_sorted = mm(perm, x_ref[0]).astype(BF)
    xp[...] = rows_sorted
    code = (index % 4) * PATCH + position
    high = in_block * (code // 64).astype(BF)
    low = in_block * (code % 64).astype(BF)
    lane_of = (kord_of % 2 * 4 + dy_of) * 16 + rank
    spread = onehot(iota((128, ROWS), 0) == lane_of)
    tags = mm_nt(high, spread) * 64.0 + mm_nt(low, spread)
    for block in range(32):
        tag_send[block] = tags[block : block + 1]

    def columns_of(rows):
        padded = jnp.concatenate(
            [rows.astype(F32), jnp.zeros((128 - rows.shape[0], 128), F32)], axis=0
        )
        return jnp.transpose(padded).astype(I32)

    row_cols = columns_of(
        jnp.concatenate([row_of[:, t * 128 : t * 128 + 128] for t in range(4)], axis=0)
    )
    for t in range(4):
        home_m[t * 128 : t * 128 + 128] = onehot(iota((128, ROWS), 1) == row_cols[:, t : t + 1])

    vobuf[:, :, 128:] = jnp.ones((2, PATCH, 128), BF)
    normed = layer_norm(rows_sorted, gain_ref[0, 0:1], shift_ref[0, 0:1])
    projected = mm(normed, qkv_ref[0]).astype(BF)
    qbuf[...] = projected[:, :WIDTH]
    kbuf[:ROWS] = projected[:, WIDTH : 2 * WIDTH]
    vobuf[0, :ROWS, :128] = projected[:, 2 * WIDTH : 2 * WIDTH + 128]
    vobuf[1, :ROWS, :128] = projected[:, 2 * WIDTH + 128 :]

    pl.semaphore_wait(barrier, PEERS)
    pair = copy_to(x_ref.at[0], px, pair_sem.at[0], pair_sem.at[1], pts=other_core)
    pair.start()

    def tag_copy(block, s, pts):
        return copy_to(tag_send.at[block], tag_recv.at[s], tag_ssem, tag_rsem, pts=pts)

    def legs(turn_index):
        first = (3 - turn_index) // 3
        last = turn_index // 3
        even = (4 + turn_index, 1 - half * first, (2 * turn_index - 1 + half) * (1 - first))
        odd = (3 - turn_index, half * last, 2 * turn_index + 1 + half * (1 - last))
        return even, odd

    for part in range(4):
        for parity, (dz, chip_half, kord) in enumerate(legs(part)):
            for dy in range(4):
                block = (2 * part + parity) * 4 + dy
                if block == 28:
                    tag_recv[28] = tag_send[28]
                else:
                    tag_copy(block, kord * 4 + dy, place(dy, dz, chip_half)).start()

    pair.wait()
    normed = layer_norm(px[...], gain_ref[0, 0:1], shift_ref[0, 0:1])
    projected = mm(normed, qkv_ref[0, :, WIDTH:]).astype(BF)
    kbuf[ROWS:] = projected[:, :WIDTH]
    vobuf[0, ROWS:, :128] = projected[:, WIDTH : WIDTH + 128]
    vobuf[1, ROWS:, :128] = projected[:, WIDTH + 128 :]

    def feed_forward(rows, block):
        normed_ff = layer_norm(rows, gain_ref[block, 1:2], shift_ref[block, 1:2])
        hidden = gelu(mm(normed_ff, up_ref[block]) + upb_ref[block : block + 1]).astype(BF)
        down = mm(hidden, down_ref[block]) + outb_ref[block, 1:2]
        return (rows.astype(F32) + down).astype(BF)

    head_lane = iota((128, 128), 1) // 16

    def part_one(part, carry):
        rows = pl.ds(pl.multiple_of(part * 128, 128), 128)
        totals = {}

        def score(step):
            group, pair_index = step
            queries = qbuf[rows, group * 128 : group * 128 + 128]
            masked = [
                jnp.where(head_lane == head, queries, jnp.zeros_like(queries))
                for head in (2 * pair_index, 2 * pair_index + 1)
            ]
            return mm_nt(
                jnp.concatenate(masked, axis=0), kbuf[:, group * 128 : group * 128 + 128]
            )

        def finish(step, scores):
            group, pair_index = step
            weights = jnp.exp2(scores * SCALE).astype(BF)
            result = mm(weights, vobuf[group])
            for side in range(2):
                mine = result[side * 128 : side * 128 + 128]
                head = 2 * pair_index + side
                if head == 0:
                    totals[group] = (mine[:, :128], mine[:, 128:])
                else:
                    top, bottom = totals[group]
                    totals[group] = (
                        jnp.where(head_lane == head, mine[:, :128], top),
                        jnp.where(head_lane == head, mine[:, 128:], bottom),
                    )

        pipelined([(g, h) for g in range(2) for h in range(4)], score, finish)
        attended = jnp.concatenate(
            [(totals[g][0] / totals[g][1]).astype(BF) for g in range(2)], axis=1
        )
        mixed = xp[rows, :].astype(F32) + (mm(attended, proj_ref[0]) + outb_ref[0, 0:1])
        send_a[rows, :] = feed_forward(mixed.astype(BF), 0)
        for parity, (dz, chip_half, kord) in enumerate(legs(part)):
            for dy in range(4):
                block = (2 * part + parity) * 4 + dy

                def start(block=block, dz=dz, chip_half=chip_half, kord=kord, dy=dy):
                    copy_to(
                        send_a.at[pl.ds(block * 16, 16)],
                        recv_a.at[pl.ds((kord * 4 + dy) * 16, 16)],
                        ab_send,
                        ab_recv.at[kord],
                        pts=place(dy, dz, chip_half),
                    ).start()

                if parity == 1 and dy == 0:
                    pl.when(part < 3)(start)
                else:
                    start()
        return carry

    lax.fori_loop(0, 4, part_one, 0)
    recv_a[448:464] = send_a[448:464]

    def wait_bytes(view, sem):
        pltpu.make_async_copy(view, view, sem).wait()

    wait_bytes(tag_recv.at[pl.ds(0, 31)], tag_rsem)
    groups = []
    for t in range(4):
        total = tag_recv[8 * t]
        for s in range(1, 8):
            total = total + tag_recv[8 * t + s]
        groups.append(total)
    tag_quad[0] = jnp.concatenate(groups + [jnp.zeros((4, 128), F32)], axis=0)
    quad_copies = [
        copy_to(
            tag_quad.at[0], tag_quad.at[rel], quad_ssem.at[rel], quad_rsem.at[rel], pts=target
        )
        for rel, target in ((1, other_chip), (2, other_core), (3, diagonal))
    ]
    for one in quad_copies:
        one.start()

    low_lane = iota((128, 128), 1) < 64
    columns = pl.multiple_of(half * 128, 128)
    mine_first = core == 0

    def project_two(rows):
        normed_two = layer_norm(rows, gain_ref[1, 0:1], shift_ref[1, 0:1])
        parts = [
            mm(normed_two, qkv_ref[1, :, pl.ds(t * WIDTH + columns, 128)]) for t in range(3)
        ]
        turned = [pltpu.roll(part, 64, 1) for part in parts]
        low = [jnp.where(mine_first, parts[t], turned[t]) for t in range(3)]
        upper = [jnp.where(mine_first, turned[t], parts[t]) for t in range(3)]
        ones = jnp.ones((128, 128), F32)
        own = [jnp.where(low_lane, low[0], upper[1]), jnp.where(low_lane, low[2], ones)]
        other = [jnp.where(low_lane, upper[0], low[1]), jnp.where(low_lane, upper[2], ones)]
        return (
            jnp.concatenate(own, axis=1).astype(BF),
            jnp.concatenate(other, axis=1).astype(BF),
        )

    def z_copy(part):
        rows = pl.ds(part * 128, 128)
        return copy_to(
            recv_a.at[rows], zrows.at[rows], z_ssem.at[part], z_rsem.at[part], pts=other_chip
        )

    def d_copy(which, part):
        rows = pl.ds(part * 128, 128)
        sem = which * 4 + part
        return copy_to(
            dsend.at[which, rows],
            gath.at[2 + which, rows],
            d_ssem.at[sem],
            d_rsem.at[sem],
            pts=other_core,
        )

    for part in range(4):
        for kord in (2 * part, 2 * part + 1):
            count = 48 if kord == 7 else 64
            wait_bytes(recv_a.at[pl.ds(kord * 64, count)], ab_recv.at[kord])
        z_copy(part).start()
    for part in range(4):
        rows = slice(part * 128, part * 128 + 128)
        gath[0, rows], dsend[0, rows] = project_two(recv_a[rows])
        d_copy(0, part).start()

    for one in quad_copies:
        one.wait_recv()
    codes = jnp.concatenate([tag_quad[rel, 0:4] for rel in range(4)], axis=0).astype(I32)
    place_in = codes // PATCH
    counts = []
    for who in range(4):
        mine = (place_in == who).astype(F32)
        mine = jnp.sum(mine, axis=1, keepdims=True)
        counts.append(jnp.sum(mine, axis=0, keepdims=True).astype(I32))
    full = [count == PATCH for count in counts]
    start_at = jnp.zeros((1, 1), I32) + PATCH
    sorted_at = codes % PATCH
    firsts = []
    for who in range(4):
        sorted_at = sorted_at + jnp.where(
            place_in == who, jnp.where(full[who], 0, start_at), 0
        )
        firsts.append(jnp.where(full[who], 0, start_at))
        start_at = start_at + jnp.where(full[who], 0, counts[who])
    zero_full = full[0]
    end_one = jnp.where(full[0], counts[1], counts[0])
    end_two = PATCH - jnp.where(full[3], counts[2], counts[3])
    cols = columns_of(sorted_at)

    for t in range(16):
        lane_row = sorted_at[t : t + 1]

        def sort_block(block, carry, t=t, lane_row=lane_row):
            rows = pl.ds(pl.multiple_of(block * 256, 256), 256)
            sort_m[rows, t * 128 : t * 128 + 128] = onehot(
                iota((256, 128), 0) + block * 256 == lane_row
            )
            return carry

        lax.fori_loop(0, 8, sort_block, 0)
        unsort_m[t * 128 : t * 128 + 128] = onehot(iota((128, 2048), 1) == cols[:, t : t + 1])

    for part in range(4):
        rows = slice(part * 128, part * 128 + 128)
        z_copy(part).wait_recv()
        gath[1, rows], dsend[1, rows] = project_two(zrows[rows])
        d_copy(1, part).start()
    for which in range(2):
        for part in range(4):
            d_copy(which, part).wait_recv()

    def sort_rows(block, carry):
        rows = pl.ds(pl.multiple_of(block * 256, 256), 256)
        total = mm(sort_m[rows, 0:512], gath[0])
        for rel in range(1, 4):
            total = total + mm(sort_m[rows, rel * 512 : rel * 512 + 512], gath[rel])
        gs[rows, :] = total.astype(BF)
        return carry

    sort_rows(0, 0)
    sort_rows(4, 0)
    cross_out[...] = jnp.where(zero_full, gs[0:CROSS], gs[PATCH : PATCH + CROSS])
    cross = copy_to(cross_out, cross_in, cross_sem.at[0], cross_sem.at[1], group=next_grp)
    cross.start()
    lax.fori_loop(1, 4, sort_rows, 0)
    lax.fori_loop(5, 8, sort_rows, 0)
    cross.wait()
    first_quad = me < 4
    in_full = jnp.logical_and(first_quad, zero_full)
    in_rest = jnp.logical_and(first_quad, jnp.logical_not(zero_full))
    gs[0:CROSS] = jnp.where(in_full, cross_in[...], gs[0:CROSS])
    gs[PATCH : PATCH + CROSS] = jnp.where(in_rest, cross_in[...], gs[PATCH : PATCH + CROSS])
    for t in range(8):
        rows = slice(t * 256, t * 256 + 256)
        kpack[rows] = pltpu.roll(gs[rows, 0:128].astype(F32), 64, 1).astype(BF)

    head_lane_two = iota((256, 128), 1) // 16

    def attend(query_rows, key_rows, mask):
        held = []

        def score(head):
            queries = gs[query_rows, 0:128]
            masked = jnp.where(head_lane_two == head, queries, jnp.zeros_like(queries))
            return mm_nt(masked, kpack[key_rows])

        def finish(head, scores):
            weights = jnp.exp2(scores * SCALE)
            if mask is not None:
                weights = jnp.where(mask, weights, 0.0)
            result = mm(weights.astype(BF), gs[key_rows, 128:256])
            if held:
                held[0] = jnp.where(head_lane_two % 4 == head, result, held[0])
            else:
                held.append(result)

        pipelined(list(range(4)), score, finish)
        total = held[0]
        attended = total / pltpu.roll(total, 64, 1)
        both = jnp.where(iota((256, 128), 1) < 64, attended, pltpu.roll(attended, 64, 1))
        att_s[query_rows] = both.astype(BF)

    def attend_full(block, carry):
        attend(pl.ds(pl.multiple_of(block * 256, 256), 256), slice(0, PATCH), None)
        return carry

    def attend_rest(block):
        low_key, high_key = ((0, 512), (0, 768), (256, 1024), (512, 1024))[block]
        size = high_key - low_key
        key_at = iota((1, size), 1) + low_key
        query_at = iota((256, 1), 0) + block * 256
        key_part = (key_at >= end_one).astype(I32) + (key_at >= end_two).astype(I32)
        query_part = (query_at >= end_one).astype(I32) + (query_at >= end_two).astype(I32)
        attend(
            slice(PATCH + block * 256, PATCH + block * 256 + 256),
            slice(PATCH + low_key, PATCH + high_key),
            query_part == key_part,
        )

    attend_full(0, 0)
    attend_rest(0)
    catt_out[...] = jnp.where(zero_full, att_s[0:CROSS], att_s[PATCH : PATCH + CROSS])
    cross_back = copy_to(catt_out, catt_in, catt_sem.at[0], catt_sem.at[1], group=last_grp)
    cross_back.start()
    lax.fori_loop(1, 4, attend_full, 0)
    for block in range(1, 4):
        attend_rest(block)
    cross_back.wait()
    att_s[0:CROSS] = jnp.where(in_full, catt_in[...], att_s[0:CROSS])
    att_s[PATCH : PATCH + CROSS] = jnp.where(
        in_rest, catt_in[...], att_s[PATCH : PATCH + CROSS]
    )

    low_lane_two = iota((256, 128), 1) < 64

    def unsorted(rel, part):
        at = rel * 512 + part * 256
        return mm(unsort_m[at : at + 256], att_s[...])

    def za_copy(part):
        rows = pl.ds(part * 256, 256)
        return copy_to(
            zatt_out.at[rows], zatt_in.at[rows], za_ssem.at[part], za_rsem.at[part], pts=other_chip
        )

    def da_copy(part):
        rows = pl.ds(part * 256, 256)
        return copy_to(
            datt_out.at[rows], datt_in.at[rows], da_ssem.at[part], da_rsem.at[part], pts=other_core
        )

    for part in range(2):
        rows = slice(part * 256, part * 256 + 256)
        zatt_out[rows] = jnp.where(low_lane_two, unsorted(1, part), unsorted(3, part)).astype(BF)
        za_copy(part).start()
    for part in range(2):
        rows = slice(part * 256, part * 256 + 256)
        for_other = unsorted(2, part)
        za_copy(part).wait_recv()
        arrived = zatt_in[rows].astype(F32)
        datt_out[rows] = jnp.where(low_lane_two, for_other, arrived).astype(BF)
        da_copy(part).start()
        own_att[rows] = jnp.where(
            low_lane_two, unsorted(0, part), pltpu.roll(arrived, 64, 1)
        ).astype(BF)

    def proj_rows(chip_half, chip_core):
        at = pl.multiple_of((chip_half * 2 + chip_core) * 64, 64)
        return proj_ref[1, pl.ds(at, 64), :]

    weights_a = jnp.concatenate([proj_rows(half, core), proj_rows(1 - half, core)], axis=0)
    weights_b = jnp.concatenate([proj_rows(half, 1 - core), proj_rows(1 - half, 1 - core)], axis=0)
    for part in range(2):
        da_copy(part).wait_recv()

    def part_two(part, carry):
        rows = pl.ds(pl.multiple_of(part * 128, 128), 128)
        out_rows = mm(own_att[rows, :], weights_a) + mm(datt_in[rows, :], weights_b)
        mixed = recv_a[rows, :].astype(F32) + (out_rows + outb_ref[1, 0:1])
        ret_send[rows, :] = feed_forward(mixed.astype(BF), 1)
        first = (3 - part) // 3
        last = part // 3
        even = (4 - part + half * (2 * part), 1 - half * first, (2 * part - 1 + half) * (1 - first))
        odd = (
            3 - part + half * (2 + 2 * part),
            half * last,
            2 * part + 1 + half * (1 - last),
        )
        for parity, (dz, chip_half, place_at) in enumerate((even, odd)):
            for dy in range(4):
                s = (2 * part + parity) * 4 + dy

                def start(s=s, dz=dz, chip_half=chip_half, place_at=place_at, dy=dy):
                    copy_to(
                        ret_send.at[pl.ds(s * 16, 16)],
                        home.at[pl.ds((place_at * 4 + dy) * 16, 16)],
                        rt_ssem,
                        rt_rsem.at[place_at],
                        pts=place(-dy, -dz, chip_half),
                    ).start()

                if parity == 1 and dy == 0:
                    pl.when(part < 3)(start)
                else:
                    start()
        return carry

    lax.fori_loop(0, 4, part_two, 0)
    home[448:464] = ret_send[448:464]
    for place_at in range(8):
        count = 48 if place_at == 7 else 64
        wait_bytes(home.at[pl.ds(place_at * 64, count)], rt_rsem.at[place_at])
    out_ref[0] = mm(home_m[...], home[...]).astype(BF)

    wait_bytes(tag_send.at[pl.ds(0, 31)], tag_ssem)
    for one in quad_copies:
        one.wait_send()
    wait_bytes(send_a.at[pl.ds(0, 496)], ab_send)
    for part in range(4):
        z_copy(part).wait_send()
    for which in range(2):
        for part in range(4):
            d_copy(which, part).wait_send()
    for part in range(2):
        za_copy(part).wait_send()
        da_copy(part).wait_send()
    wait_bytes(ret_send.at[pl.ds(0, 496)], rt_ssem)


def on_device(
    features,
    hilbert_slot,
    hilbert_count,
    norm_gain,
    norm_shift,
    qkv_weight,
    proj_weight,
    up_weight,
    up_bias,
    down_weight,
    out_bias,
):
    vmem = pl.BlockSpec(memory_space=pltpu.VMEM)
    sems = pltpu.SemaphoreType.DMA
    rows_buffer = pltpu.VMEM((ROWS, WIDTH), BF)
    half_buffer = pltpu.VMEM((ROWS, 128), BF)
    scratch = [
        rows_buffer,
        rows_buffer,
        rows_buffer,
        pltpu.VMEM((PATCH, WIDTH), BF),
        pltpu.VMEM((2, PATCH, WIDTH), BF),
        rows_buffer,
        rows_buffer,
        pltpu.VMEM((32, 1, 128), F32),
        pltpu.VMEM((32, 1, 128), F32),
        pltpu.VMEM((4, 8, 128), F32),
        rows_buffer,
        pltpu.VMEM((4, ROWS, WIDTH), BF),
        pltpu.VMEM((2, ROWS, WIDTH), BF),
        pltpu.VMEM((2 * PATCH, 2 * PATCH), BF),
        pltpu.VMEM((2 * PATCH, 2 * PATCH), BF),
        pltpu.VMEM((ROWS, ROWS), BF),
        pltpu.VMEM((2 * PATCH, WIDTH), BF),
        pltpu.VMEM((2 * PATCH, 128), BF),
        pltpu.VMEM((CROSS, WIDTH), BF),
        pltpu.VMEM((CROSS, WIDTH), BF),
        pltpu.VMEM((2 * PATCH, 128), BF),
        pltpu.VMEM((CROSS, 128), BF),
        pltpu.VMEM((CROSS, 128), BF),
        half_buffer,
        half_buffer,
        half_buffer,
        half_buffer,
        half_buffer,
        rows_buffer,
        rows_buffer,
        sems,
        sems((8,)),
        sems,
        sems,
        sems((4,)),
        sems((4,)),
        sems((2,)),
        sems((4,)),
        sems((4,)),
        sems((8,)),
        sems((8,)),
        sems((2,)),
        sems((2,)),
        sems((2,)),
        sems((2,)),
        sems((2,)),
        sems((2,)),
        sems,
        sems((8,)),
    ]
    return pl.pallas_call(
        kernel,
        out_shape=jax.ShapeDtypeStruct((1, ROWS, WIDTH), BF),
        in_specs=[vmem] * 10,
        out_specs=vmem,
        scratch_shapes=scratch,
        compiler_params=pltpu.CompilerParams(
            collective_id=0, has_side_effects=True, vmem_limit_bytes=60 * 2**20
        ),
    )(
        features,
        hilbert_slot,
        norm_gain,
        norm_shift,
        qkv_weight,
        proj_weight,
        up_weight,
        up_bias,
        down_weight,
        out_bias,
    )


def solution(mesh):
    return jax.shard_map(
        on_device,
        mesh=mesh,
        in_specs=(
            P("grp", "pts", None),
            P("grp", "pts"),
            P("grp", "pts"),
            P(),
            P(),
            P(),
            P(),
            P(),
            P(),
            P(),
            P(),
        ),
        out_specs=P("grp", "pts", None),
        check_vma=False,
    )
```

```python
import functools

import jax
import jax.numpy as jnp
from jax import lax
from jax.experimental import pallas as pl
from jax.experimental.pallas import tpu as pltpu
from jax.sharding import PartitionSpec as P

BF = jnp.bfloat16
F32 = jnp.float32
I32 = jnp.int32
MESH = pl.DeviceIdType.MESH
NORM_EPS = 1e-05
SCALE = 0.25 * 1.4426950408889634
ROWS = 512
WIDTH = 256
PATCH = 1024
CROSS = 64
PEERS = 48


def layer_norm(rows, gain, shift):
    rows = rows.astype(F32)
    centered = rows - jnp.mean(rows, axis=-1, keepdims=True)
    spread = jnp.mean(centered * centered, axis=-1, keepdims=True)
    return (centered * lax.rsqrt(spread + NORM_EPS) * gain + shift).astype(BF)


def mm(left, right):
    return jnp.dot(left, right, preferred_element_type=F32)


def mm_nt(left, right):
    return lax.dot_general(left, right, (((1,), (1,)), ((), ())), preferred_element_type=F32)


def iota(shape, dim):
    return lax.broadcasted_iota(I32, shape, dim)


def onehot(mask):
    return jnp.where(mask, 1.0, 0.0).astype(BF)


def gelu(values):
    return 0.5 * values * (1.0 + lax.erf(values * 0.7071067811865476))


def pipelined(parts, score, finish):
    scores = score(parts[0])
    for index, part in enumerate(parts):
        ahead = score(parts[index + 1]) if index + 1 < len(parts) else None
        finish(part, scores)
        scores = ahead


def kernel(
    x_ref,
    slot_ref,
    gain_ref,
    shift_ref,
    qkv_any,
    proj_any,
    up_any,
    upb_ref,
    down_any,
    outb_ref,
    out_ref,
    qkv_ref,
    proj_ref,
    up_ref,
    down_ref,
    weight_sem,
    px,
    xp,
    acc,
    qbuf,
    kbuf,
    vobuf,
    send_a,
    recv_a,
    tag_send,
    tag_recv,
    tag_quad,
    zrows,
    gath,
    dsend,
    sort_m,
    unsort_m,
    home_m,
    gacc,
    gs,
    kpack,
    cross_out,
    cross_in,
    att_s,
    catt_out,
    catt_in,
    zatt_out,
    zatt_in,
    own_att,
    other_att,
    datt_out,
    datt_in,
    ret_send,
    home,
    ab_send,
    ab_recv,
    tag_ssem,
    tag_rsem,
    quad_ssem,
    quad_rsem,
    pair_sem,
    z_ssem,
    z_rsem,
    d_ssem,
    d_rsem,
    cross_sem,
    catt_sem,
    za_ssem,
    za_rsem,
    da_ssem,
    da_rsem,
    rt_ssem,
    rt_rsem,
):
    me = lax.axis_index("pts")
    grp = lax.axis_index("grp")
    core = me % 2
    half = (me // 2) % 2
    quad_z = (me // 4) % 8
    quad_y = me // 32
    base = me // 4 * 4
    other_core = base + half * 2 + (1 - core)
    other_chip = base + (1 - half) * 2 + core
    diagonal = base + (1 - half) * 2 + (1 - core)
    next_grp = (grp + 1) % 4
    last_grp = (grp + 3) % 4

    def place(dy, dz, chip_half):
        return (((quad_y + dy + 4) % 4) * 8 + (quad_z + dz + 8) % 8) * 4 + chip_half * 2 + core

    def copy_to(src, dst, ssem, rsem, pts=None, group=None):
        target = {"pts": pts} if group is None else {"grp": group}
        return pltpu.make_async_remote_copy(
            src_ref=src,
            dst_ref=dst,
            send_sem=ssem,
            recv_sem=rsem,
            device_id=target,
            device_id_type=MESH,
        )

    def wait_bytes(view, sem):
        pltpu.make_async_copy(view, view, sem).wait()

    barrier = pltpu.get_barrier_semaphore()

    def greet(target):
        pl.semaphore_signal(barrier, inc=1, device_id=target, device_id_type=MESH)

    for dy in range(4):
        for dz in range(1, 4):
            greet({"pts": place(dy, dz, 0)})
            greet({"pts": place(dy, 8 - dz, 1)})
            greet({"pts": place(dy, (8 - dz) * (1 - half) + dz * half, half)})
        greet({"pts": place(dy, 4, 1 - half)})
        if dy:
            greet({"pts": place(dy, 0, half)})
    greet({"pts": other_core})
    greet({"pts": other_chip})
    greet({"pts": diagonal})
    greet({"grp": next_grp})
    greet({"grp": last_grp})

    loads = [
        pltpu.make_async_copy(source, target, weight_sem.at[index])
        for index, (source, target) in enumerate(
            (
                (qkv_any, qkv_ref),
                (proj_any, proj_ref),
                (up_any, up_ref),
                (down_any, down_ref),
            )
        )
    ]
    for one in loads:
        one.start()

    slot = slot_ref[...]
    owner = slot // PATCH
    position = slot % PATCH
    index = jnp.where(owner // 128 == grp, owner % 128, 0)
    quad = index // 4
    dy_of = (quad // 8 - quad_y + 4) % 4
    dz_of = (quad % 8 - quad_z + 8) % 8
    turn = dz_of - 4
    place_of = 2 * jnp.abs(turn) - (turn < 0).astype(I32)
    block_of = place_of * 4 + dy_of
    inner = jnp.where(place_of % 2 == 1, place_of + half, place_of - 1 + half)
    kord_of = jnp.where(place_of == 0, 0, jnp.where(place_of == 7, 7, inner))
    in_block = onehot(iota((32, ROWS), 0) == block_of)
    upto = onehot(iota((ROWS, ROWS), 0) <= iota((ROWS, ROWS), 1))
    counted = mm(in_block, upto)
    rank = jnp.sum(in_block.astype(F32) * counted, axis=0, keepdims=True).astype(I32) - 1
    row_of = block_of * 16 + rank
    perm = onehot(iota((ROWS, ROWS), 0) == row_of)
    rows_sorted = mm(perm, x_ref[0]).astype(BF)
    xp[...] = rows_sorted
    code = (index % 4) * PATCH + position
    high = in_block * (code // 64).astype(BF)
    low = in_block * (code % 64).astype(BF)
    lane_of = (kord_of % 2 * 4 + dy_of) * 16 + rank
    spread = onehot(iota((128, ROWS), 0) == lane_of)
    tags = mm_nt(high, spread) * 64.0 + mm_nt(low, spread)
    for block in range(32):
        tag_send[block] = tags[block : block + 1]

    def columns_of(rows):
        padded = jnp.concatenate(
            [rows.astype(F32), jnp.zeros((128 - rows.shape[0], 128), F32)], axis=0
        )
        return jnp.transpose(padded).astype(I32)

    vobuf[:, :, 128:] = jnp.ones((2, PATCH, 128), BF)
    loads[0].wait()
    normed = layer_norm(rows_sorted, gain_ref[0, 0:1], shift_ref[0, 0:1])
    projected = mm(normed, qkv_ref[0]).astype(BF)
    qbuf[...] = projected[:, :WIDTH]
    kbuf[:ROWS] = projected[:, WIDTH : 2 * WIDTH]
    vobuf[0, :ROWS, :128] = projected[:, 2 * WIDTH : 2 * WIDTH + 128]
    vobuf[1, :ROWS, :128] = projected[:, 2 * WIDTH + 128 :]

    def feed_forward(rows, block):
        normed_ff = layer_norm(rows, gain_ref[block, 1:2], shift_ref[block, 1:2])
        hidden = gelu(mm(normed_ff, up_ref[block]) + upb_ref[block : block + 1]).astype(BF)
        down = mm(hidden, down_ref[block]) + outb_ref[block, 1:2]
        return (rows.astype(F32) + down).astype(BF)

    head_lane = iota((128, 128), 1) // 16

    def attend_one(rows, keys):
        totals = {}

        def score(step):
            group, pair_index = step
            queries = qbuf[rows, group * 128 : group * 128 + 128]
            masked = [
                jnp.where(head_lane == head, queries, jnp.zeros_like(queries))
                for head in (2 * pair_index, 2 * pair_index + 1)
            ]
            return mm_nt(
                jnp.concatenate(masked, axis=0), kbuf[keys, group * 128 : group * 128 + 128]
            )

        def finish(step, scores):
            group, pair_index = step
            weights = jnp.exp2(scores * SCALE).astype(BF)
            result = mm(weights, vobuf[group, keys])
            for side in range(2):
                mine = result[side * 128 : side * 128 + 128]
                head = 2 * pair_index + side
                if head == 0:
                    totals[group] = (mine[:, :128], mine[:, 128:])
                else:
                    top, bottom = totals[group]
                    totals[group] = (
                        jnp.where(head_lane == head, mine[:, :128], top),
                        jnp.where(head_lane == head, mine[:, 128:], bottom),
                    )

        pipelined([(g, h) for g in range(2) for h in range(4)], score, finish)
        return totals

    def own_keys(part, carry):
        rows = pl.ds(pl.multiple_of(part * 128, 128), 128)
        totals = attend_one(rows, slice(0, ROWS))
        for group in range(2):
            acc[rows, group * 256 : group * 256 + 128] = totals[group][0]
            acc[rows, group * 256 + 128 : group * 256 + 256] = totals[group][1]
        return carry

    lax.fori_loop(0, 3, own_keys, 0)
    pl.semaphore_wait(barrier, PEERS)
    pair = copy_to(x_ref.at[0], px, pair_sem.at[0], pair_sem.at[1], pts=other_core)
    pair.start()

    def tag_copy(block, s, pts):
        return copy_to(tag_send.at[block], tag_recv.at[s], tag_ssem, tag_rsem, pts=pts)

    def legs(turn_index):
        first = (3 - turn_index) // 3
        last = turn_index // 3
        even = (4 + turn_index, 1 - half * first, (2 * turn_index - 1 + half) * (1 - first))
        odd = (3 - turn_index, half * last, 2 * turn_index + 1 + half * (1 - last))
        return even, odd

    for part in range(4):
        for parity, (dz, chip_half, kord) in enumerate(legs(part)):
            for dy in range(4):
                block = (2 * part + parity) * 4 + dy
                if block == 28:
                    tag_recv[28] = tag_send[28]
                else:
                    tag_copy(block, kord * 4 + dy, place(dy, dz, chip_half)).start()

    lax.fori_loop(3, 4, own_keys, 0)
    for one in loads[1:]:
        one.wait()
    pair.wait()
    normed = layer_norm(px[...], gain_ref[0, 0:1], shift_ref[0, 0:1])
    projected = mm(normed, qkv_ref[0, :, WIDTH:]).astype(BF)
    kbuf[ROWS:] = projected[:, :WIDTH]
    vobuf[0, ROWS:, :128] = projected[:, WIDTH : WIDTH + 128]
    vobuf[1, ROWS:, :128] = projected[:, WIDTH + 128 :]


    quad_copies = [
        copy_to(
            tag_quad.at[0], tag_quad.at[rel], quad_ssem.at[rel], quad_rsem.at[rel], pts=target
        )
        for rel, target in ((1, other_chip), (2, other_core), (3, diagonal))
    ]

    def share_tags():
        wait_bytes(tag_recv.at[pl.ds(0, 31)], tag_rsem)
        groups = []
        for t in range(4):
            total = tag_recv[8 * t]
            for s in range(1, 8):
                total = total + tag_recv[8 * t + s]
            groups.append(total)
        tag_quad[0] = jnp.concatenate(groups + [jnp.zeros((4, 128), F32)], axis=0)
        for one in quad_copies:
            one.start()

    def part_one(part, carry):
        rows = pl.ds(pl.multiple_of(part * 128, 128), 128)
        totals = attend_one(rows, slice(ROWS, PATCH))
        tops = [acc[rows, g * 256 : g * 256 + 128] + totals[g][0] for g in range(2)]
        bottoms = [acc[rows, g * 256 + 128 : g * 256 + 256] + totals[g][1] for g in range(2)]
        attended = jnp.concatenate(
            [(tops[g] / bottoms[g]).astype(BF) for g in range(2)], axis=1
        )
        mixed = xp[rows, :].astype(F32) + (mm(attended, proj_ref[0]) + outb_ref[0, 0:1])
        send_a[rows, :] = feed_forward(mixed.astype(BF), 0)
        for parity, (dz, chip_half, kord) in enumerate(legs(part)):
            for dy in range(4):
                block = (2 * part + parity) * 4 + dy

                def start(block=block, dz=dz, chip_half=chip_half, kord=kord, dy=dy):
                    copy_to(
                        send_a.at[pl.ds(block * 16, 16)],
                        recv_a.at[pl.ds((kord * 4 + dy) * 16, 16)],
                        ab_send,
                        ab_recv.at[kord],
                        pts=place(dy, dz, chip_half),
                    ).start()

                if parity == 1 and dy == 0:
                    pl.when(part < 3)(start)
                else:
                    start()
        pl.when(part == 1)(share_tags)
        return carry

    lax.fori_loop(0, 4, part_one, 0)
    recv_a[448:464] = send_a[448:464]

    low_lane = iota((128, 128), 1) < 64
    columns = pl.multiple_of(half * 128, 128)
    mine_first = core == 0

    def project_two(rows):
        normed_two = layer_norm(rows, gain_ref[1, 0:1], shift_ref[1, 0:1])
        parts = [
            mm(normed_two, qkv_ref[1, :, pl.ds(t * WIDTH + columns, 128)]) for t in range(3)
        ]
        turned = [pltpu.roll(part, 64, 1) for part in parts]
        low = [jnp.where(mine_first, parts[t], turned[t]) for t in range(3)]
        upper = [jnp.where(mine_first, turned[t], parts[t]) for t in range(3)]
        ones = jnp.ones((128, 128), F32)
        own = [jnp.where(low_lane, low[0], upper[1]), jnp.where(low_lane, low[2], ones)]
        other = [jnp.where(low_lane, upper[0], low[1]), jnp.where(low_lane, upper[2], ones)]
        return (
            jnp.concatenate(own, axis=1).astype(BF),
            jnp.concatenate(other, axis=1).astype(BF),
        )

    def z_copy(part):
        rows = pl.ds(part * 128, 128)
        return copy_to(
            recv_a.at[rows], zrows.at[rows], z_ssem.at[part], z_rsem.at[part], pts=other_chip
        )

    def d_copy(which, part):
        rows = pl.ds(part * 128, 128)
        sem = which * 4 + part
        return copy_to(
            dsend.at[which, rows],
            gath.at[2 + which, rows],
            d_ssem.at[sem],
            d_rsem.at[sem],
            pts=other_core,
        )

    for one in quad_copies:
        one.wait_recv()
    codes = jnp.concatenate([tag_quad[rel, 0:4] for rel in range(4)], axis=0).astype(I32)
    place_in = codes // PATCH
    counts = []
    for who in range(4):
        mine = (place_in == who).astype(F32)
        mine = jnp.sum(mine, axis=1, keepdims=True)
        counts.append(jnp.sum(mine, axis=0, keepdims=True).astype(I32))
    full = [count == PATCH for count in counts]
    start_at = jnp.zeros((1, 1), I32) + PATCH
    sorted_at = codes % PATCH
    firsts = []
    for who in range(4):
        sorted_at = sorted_at + jnp.where(
            place_in == who, jnp.where(full[who], 0, start_at), 0
        )
        firsts.append(jnp.where(full[who], 0, start_at))
        start_at = start_at + jnp.where(full[who], 0, counts[who])
    zero_full = full[0]
    end_one = jnp.where(full[0], counts[1], counts[0])
    end_two = PATCH - jnp.where(full[3], counts[2], counts[3])
    cols = columns_of(sorted_at)

    def build_onehots(t):
        lane_row = sorted_at[t : t + 1]

        def sort_block(block, carry):
            rows = pl.ds(pl.multiple_of(block * 256, 256), 256)
            sort_m[rows, t * 128 : t * 128 + 128] = onehot(
                iota((256, 128), 0) + block * 256 == lane_row
            )
            return carry

        lax.fori_loop(0, 8, sort_block, 0)
        unsort_m[t * 128 : t * 128 + 128] = onehot(iota((128, 2048), 1) == cols[:, t : t + 1])

    for part in range(4):
        for t in range(4 * part, 4 * part + 4):
            build_onehots(t)
        for kord in (2 * part, 2 * part + 1):
            count = 48 if kord == 7 else 64
            wait_bytes(recv_a.at[pl.ds(kord * 64, count)], ab_recv.at[kord])
        z_copy(part).start()
        rows = slice(part * 128, part * 128 + 128)
        gath[0, rows], dsend[0, rows] = project_two(recv_a[rows])
        d_copy(0, part).start()

    def partner_rows(part):
        rows = slice(part * 128, part * 128 + 128)
        z_copy(part).wait_recv()
        gath[1, rows], dsend[1, rows] = project_two(zrows[rows])
        d_copy(1, part).start()

    def sort_some(rows, rels):
        total = mm(sort_m[rows, rels[0] * 512 : rels[0] * 512 + 512], gath[rels[0]])
        for rel in rels[1:]:
            total = total + mm(sort_m[rows, rel * 512 : rel * 512 + 512], gath[rel])
        return total

    def sort_own(block, carry):
        rows = pl.ds(pl.multiple_of(block * 256, 256), 256)
        gacc[rows, :] = sort_some(rows, (0, 2))
        return carry

    partner_rows(0)
    partner_rows(1)
    for part in range(4):
        d_copy(0, part).wait_recv()
    lax.fori_loop(0, 8, sort_own, 0)
    partner_rows(2)
    partner_rows(3)
    for part in range(4):
        d_copy(1, part).wait_recv()

    def sort_rows(block, carry):
        rows = pl.ds(pl.multiple_of(block * 256, 256), 256)
        total = gacc[rows, :] + sort_some(rows, (1, 3))
        gs[rows, :] = total.astype(BF)
        kpack[rows, :] = pltpu.roll(total[:, 0:128], 64, 1).astype(BF)
        return carry

    sort_rows(0, 0)
    sort_rows(4, 0)
    cross_out[...] = jnp.where(zero_full, gs[0:CROSS], gs[PATCH : PATCH + CROSS])
    cross = copy_to(cross_out, cross_in, cross_sem.at[0], cross_sem.at[1], group=next_grp)
    cross.start()
    lax.fori_loop(1, 4, sort_rows, 0)
    lax.fori_loop(5, 8, sort_rows, 0)
    cross.wait()
    first_quad = me < 4
    in_full = jnp.logical_and(first_quad, zero_full)
    in_rest = jnp.logical_and(first_quad, jnp.logical_not(zero_full))
    gs[0:CROSS] = jnp.where(in_full, cross_in[...], gs[0:CROSS])
    gs[PATCH : PATCH + CROSS] = jnp.where(in_rest, cross_in[...], gs[PATCH : PATCH + CROSS])
    for rows in (slice(0, CROSS), slice(PATCH, PATCH + CROSS)):
        kpack[rows] = pltpu.roll(gs[rows, 0:128].astype(F32), 64, 1).astype(BF)

    head_lane_two = iota((256, 128), 1) // 16

    def attend(query_rows, key_rows, mask):
        held = []

        def score(head):
            queries = gs[query_rows, 0:128]
            masked = jnp.where(head_lane_two == head, queries, jnp.zeros_like(queries))
            return mm_nt(masked, kpack[key_rows])

        def finish(head, scores):
            weights = jnp.exp2(scores * SCALE)
            if mask is not None:
                weights = jnp.where(mask, weights, 0.0)
            result = mm(weights.astype(BF), gs[key_rows, 128:256])
            if held:
                held[0] = jnp.where(head_lane_two % 4 == head, result, held[0])
            else:
                held.append(result)

        pipelined(list(range(4)), score, finish)
        total = held[0]
        attended = total / pltpu.roll(total, 64, 1)
        both = jnp.where(iota((256, 128), 1) < 64, attended, pltpu.roll(attended, 64, 1))
        att_s[query_rows] = both.astype(BF)

    def attend_full(block, carry):
        attend(pl.ds(pl.multiple_of(block * 256, 256), 256), slice(0, PATCH), None)
        return carry

    def attend_rest(block):
        low_key, high_key = ((0, 512), (0, 768), (256, 1024), (512, 1024))[block]
        size = high_key - low_key
        key_at = iota((1, size), 1) + low_key
        query_at = iota((256, 1), 0) + block * 256
        key_part = (key_at >= end_one).astype(I32) + (key_at >= end_two).astype(I32)
        query_part = (query_at >= end_one).astype(I32) + (query_at >= end_two).astype(I32)
        attend(
            slice(PATCH + block * 256, PATCH + block * 256 + 256),
            slice(PATCH + low_key, PATCH + high_key),
            query_part == key_part,
        )

    attend_full(0, 0)
    attend_rest(0)
    catt_out[...] = jnp.where(zero_full, att_s[0:CROSS], att_s[PATCH : PATCH + CROSS])
    cross_back = copy_to(catt_out, catt_in, catt_sem.at[0], catt_sem.at[1], group=last_grp)
    cross_back.start()
    lax.fori_loop(1, 4, attend_full, 0)
    for block in range(1, 4):
        attend_rest(block)
    cross_back.wait()
    att_s[0:CROSS] = jnp.where(in_full, catt_in[...], att_s[0:CROSS])
    att_s[PATCH : PATCH + CROSS] = jnp.where(
        in_rest, catt_in[...], att_s[PATCH : PATCH + CROSS]
    )

    def unsorted(rel, at, size):
        return mm(unsort_m[rel * 512 + at : rel * 512 + at + size], att_s[...])

    def za_copy(part):
        rows = pl.ds(part * 128, 128)
        return copy_to(
            zatt_out.at[rows], zatt_in.at[rows], za_ssem.at[part], za_rsem.at[part], pts=other_chip
        )

    def da_copy(part):
        rows = pl.ds(part * 128, 128)
        return copy_to(
            datt_out.at[rows], datt_in.at[rows], da_ssem.at[part], da_rsem.at[part], pts=other_core
        )

    low_lane_two = iota((256, 128), 1) < 64
    for part in range(2):
        rows = slice(part * 256, part * 256 + 256)
        zatt_out[rows] = jnp.where(
            low_lane_two, unsorted(1, part * 256, 256), unsorted(3, part * 256, 256)
        ).astype(BF)
        za_copy(2 * part).start()
        za_copy(2 * part + 1).start()
    other_att[...] = unsorted(2, 0, ROWS)
    own_att[...] = unsorted(0, 0, ROWS).astype(BF)

    def proj_rows(chip_half, chip_core):
        at = pl.multiple_of((chip_half * 2 + chip_core) * 64, 64)
        return proj_ref[1, pl.ds(at, 64), :]

    weights_a = jnp.concatenate([proj_rows(half, core), proj_rows(1 - half, core)], axis=0)
    weights_b = jnp.concatenate([proj_rows(half, 1 - core), proj_rows(1 - half, 1 - core)], axis=0)

    def regroup(part):
        rows = pl.ds(pl.multiple_of(part * 128, 128), 128)
        za_copy(part).wait_recv()
        arrived = zatt_in[rows, :].astype(F32)
        datt_out[rows, :] = jnp.where(low_lane, other_att[rows, :], arrived).astype(BF)
        da_copy(part).start()
        own_att[rows, :] = jnp.where(
            low_lane, own_att[rows, :], pltpu.roll(arrived, 64, 1).astype(BF)
        )

    def part_two(part):
        rows = pl.ds(pl.multiple_of(part * 128, 128), 128)
        da_copy(part).wait_recv()
        out_rows = mm(own_att[rows, :], weights_a) + mm(datt_in[rows, :], weights_b)
        mixed = recv_a[rows, :].astype(F32) + (out_rows + outb_ref[1, 0:1])
        ret_send[rows, :] = feed_forward(mixed.astype(BF), 1)
        first = (3 - part) // 3
        last = part // 3
        even = (4 - part + half * (2 * part), 1 - half * first, (2 * part - 1 + half) * (1 - first))
        odd = (
            3 - part + half * (2 + 2 * part),
            half * last,
            2 * part + 1 + half * (1 - last),
        )
        for parity, (dz, chip_half, place_at) in enumerate((even, odd)):
            for dy in range(4):
                s = (2 * part + parity) * 4 + dy

                def start(s=s, dz=dz, chip_half=chip_half, place_at=place_at, dy=dy):
                    copy_to(
                        ret_send.at[pl.ds(s * 16, 16)],
                        home.at[pl.ds((place_at * 4 + dy) * 16, 16)],
                        rt_ssem,
                        rt_rsem.at[place_at],
                        pts=place(-dy, -dz, chip_half),
                    ).start()

                if parity == 1 and dy == 0:
                    pl.when(part < 3)(start)
                else:
                    start()

    def return_step(step, carry):
        pl.when(step < 4)(lambda: regroup(step))
        pl.when(step > 0)(lambda: part_two(step - 1))
        return carry

    lax.fori_loop(0, 5, return_step, 0)
    row_cols = columns_of(
        jnp.concatenate([row_of[:, t * 128 : t * 128 + 128] for t in range(4)], axis=0)
    )
    for t in range(4):
        home_m[t * 128 : t * 128 + 128] = onehot(iota((128, ROWS), 1) == row_cols[:, t : t + 1])
    home[448:464] = ret_send[448:464]
    for place_at in range(8):
        count = 48 if place_at == 7 else 64
        wait_bytes(home.at[pl.ds(place_at * 64, count)], rt_rsem.at[place_at])
    out_ref[0] = mm(home_m[...], home[...]).astype(BF)

    wait_bytes(tag_send.at[pl.ds(0, 31)], tag_ssem)
    for one in quad_copies:
        one.wait_send()
    wait_bytes(send_a.at[pl.ds(0, 496)], ab_send)
    for part in range(4):
        z_copy(part).wait_send()
    for which in range(2):
        for part in range(4):
            d_copy(which, part).wait_send()
    for part in range(4):
        za_copy(part).wait_send()
        da_copy(part).wait_send()
    wait_bytes(ret_send.at[pl.ds(0, 496)], rt_ssem)


def on_device(
    features,
    hilbert_slot,
    hilbert_count,
    norm_gain,
    norm_shift,
    qkv_weight,
    proj_weight,
    up_weight,
    up_bias,
    down_weight,
    out_bias,
):
    vmem = pl.BlockSpec(memory_space=pltpu.VMEM)
    sems = pltpu.SemaphoreType.DMA
    rows_buffer = pltpu.VMEM((ROWS, WIDTH), BF)
    half_buffer = pltpu.VMEM((ROWS, 128), BF)
    any_space = pl.BlockSpec(memory_space=pl.ANY)
    scratch = [
        pltpu.VMEM((2, WIDTH, 3 * WIDTH), BF),
        pltpu.VMEM((2, WIDTH, WIDTH), BF),
        pltpu.VMEM((2, WIDTH, 4 * WIDTH), BF),
        pltpu.VMEM((2, 4 * WIDTH, WIDTH), BF),
        sems((4,)),
        rows_buffer,
        rows_buffer,
        pltpu.VMEM((ROWS, 2 * WIDTH), F32),
        rows_buffer,
        pltpu.VMEM((PATCH, WIDTH), BF),
        pltpu.VMEM((2, PATCH, WIDTH), BF),
        rows_buffer,
        rows_buffer,
        pltpu.VMEM((32, 1, 128), F32),
        pltpu.VMEM((32, 1, 128), F32),
        pltpu.VMEM((4, 8, 128), F32),
        rows_buffer,
        pltpu.VMEM((4, ROWS, WIDTH), BF),
        pltpu.VMEM((2, ROWS, WIDTH), BF),
        pltpu.VMEM((2 * PATCH, 2 * PATCH), BF),
        pltpu.VMEM((2 * PATCH, 2 * PATCH), BF),
        pltpu.VMEM((ROWS, ROWS), BF),
        pltpu.VMEM((2 * PATCH, WIDTH), F32),
        pltpu.VMEM((2 * PATCH, WIDTH), BF),
        pltpu.VMEM((2 * PATCH, 128), BF),
        pltpu.VMEM((CROSS, WIDTH), BF),
        pltpu.VMEM((CROSS, WIDTH), BF),
        pltpu.VMEM((2 * PATCH, 128), BF),
        pltpu.VMEM((CROSS, 128), BF),
        pltpu.VMEM((CROSS, 128), BF),
        half_buffer,
        half_buffer,
        half_buffer,
        pltpu.VMEM((ROWS, 128), F32),
        half_buffer,
        half_buffer,
        rows_buffer,
        rows_buffer,
        sems,
        sems((8,)),
        sems,
        sems,
        sems((4,)),
        sems((4,)),
        sems((2,)),
        sems((4,)),
        sems((4,)),
        sems((8,)),
        sems((8,)),
        sems((2,)),
        sems((2,)),
        sems((4,)),
        sems((4,)),
        sems((4,)),
        sems((4,)),
        sems,
        sems((8,)),
    ]
    return pl.pallas_call(
        kernel,
        out_shape=jax.ShapeDtypeStruct((1, ROWS, WIDTH), BF),
        in_specs=[vmem] * 4 + [any_space] * 3 + [vmem, any_space, vmem],
        out_specs=vmem,
        scratch_shapes=scratch,
        compiler_params=pltpu.CompilerParams(
            collective_id=0, has_side_effects=True, vmem_limit_bytes=60 * 2**20
        ),
    )(
        features,
        hilbert_slot,
        norm_gain,
        norm_shift,
        qkv_weight,
        proj_weight,
        up_weight,
        up_bias,
        down_weight,
        out_bias,
    )


def solution(mesh):
    return jax.shard_map(
        on_device,
        mesh=mesh,
        in_specs=(
            P("grp", "pts", None),
            P("grp", "pts"),
            P("grp", "pts"),
            P(),
            P(),
            P(),
            P(),
            P(),
            P(),
            P(),
            P(),
        ),
        out_specs=P("grp", "pts", None),
        check_vma=False,
    )
```

```python
import functools

import jax
import jax.numpy as jnp
from jax import lax
from jax.experimental import pallas as pl
from jax.experimental.pallas import tpu as pltpu
from jax.sharding import PartitionSpec as P

BF = jnp.bfloat16
F32 = jnp.float32
I32 = jnp.int32
MESH = pl.DeviceIdType.MESH
NORM_EPS = 1e-05
LOG2E = 1.4426950408889634
SCALE = 0.25 * LOG2E
ROWS = 512
WIDTH = 256
PATCH = 1024
CROSS = 64
PEERS = 48


def layer_norm(rows, gain, shift):
    rows = rows.astype(F32)
    centered = rows - jnp.mean(rows, axis=-1, keepdims=True)
    spread = jnp.mean(centered * centered, axis=-1, keepdims=True)
    return (centered * lax.rsqrt(spread + NORM_EPS) * gain + shift).astype(BF)


def mm(left, right):
    return jnp.dot(left, right, preferred_element_type=F32)


def mm_nt(left, right):
    return lax.dot_general(left, right, (((1,), (1,)), ((), ())), preferred_element_type=F32)


def iota(shape, dim):
    return lax.broadcasted_iota(I32, shape, dim)


def onehot(mask):
    return jnp.where(mask, 1.0, 0.0).astype(BF)


def gelu(values):
    size = jnp.abs(values)
    under = 1.0 + 0.23164189 * size
    t = pl.reciprocal(under, approx=True)
    t = t * (2.0 - under * t)
    poly = 0.5 * 1.061405429 * t - 0.5 * 1.453152027
    for factor in (0.5 * 1.421413741, -0.5 * 0.284496736, 0.5 * 0.254829592):
        poly = poly * t + factor
    tail = jnp.exp2(values * values * (-0.5 * LOG2E)) * (poly * t)
    return jnp.maximum(values, 0.0) - size * tail


def pipelined(parts, score, finish):
    scores = score(parts[0])
    for index, part in enumerate(parts):
        ahead = score(parts[index + 1]) if index + 1 < len(parts) else None
        finish(part, scores)
        scores = ahead


def kernel(
    x_ref,
    slot_ref,
    gain_ref,
    shift_ref,
    qkv_any,
    proj_any,
    up_any,
    upb_ref,
    down_any,
    outb_ref,
    out_ref,
    qkv_ref,
    proj_ref,
    up_ref,
    down_ref,
    weight_sem,
    px,
    xp,
    acc,
    qbuf,
    kbuf,
    vobuf,
    send_a,
    recv_a,
    tag_send,
    tag_recv,
    tag_quad,
    zrows,
    gath,
    dsend,
    sort_m,
    unsort_m,
    home_m,
    gacc,
    gs,
    kpack,
    cross_out,
    cross_in,
    att_s,
    catt_out,
    catt_in,
    att_out,
    att_in,
    wide_proj,
    ret_send,
    home,
    ab_send,
    ab_recv,
    tag_ssem,
    tag_rsem,
    quad_ssem,
    quad_rsem,
    pair_sem,
    z_ssem,
    z_rsem,
    d_ssem,
    d_rsem,
    cross_sem,
    catt_sem,
    at_ssem,
    at_rsem,
    rt_ssem,
    rt_rsem,
):
    me = lax.axis_index("pts")
    grp = lax.axis_index("grp")
    core = me % 2
    half = (me // 2) % 2
    quad_z = (me // 4) % 8
    quad_y = me // 32
    base = me // 4 * 4
    other_core = base + half * 2 + (1 - core)
    other_chip = base + (1 - half) * 2 + core
    diagonal = base + (1 - half) * 2 + (1 - core)
    next_grp = (grp + 1) % 4
    last_grp = (grp + 3) % 4

    def place(dy, dz, chip_half):
        return (((quad_y + dy + 4) % 4) * 8 + (quad_z + dz + 8) % 8) * 4 + chip_half * 2 + core

    def copy_to(src, dst, ssem, rsem, pts=None, group=None):
        target = {"pts": pts} if group is None else {"grp": group}
        return pltpu.make_async_remote_copy(
            src_ref=src,
            dst_ref=dst,
            send_sem=ssem,
            recv_sem=rsem,
            device_id=target,
            device_id_type=MESH,
        )

    def wait_bytes(view, sem):
        pltpu.make_async_copy(view, view, sem).wait()

    barrier = pltpu.get_barrier_semaphore()

    def greet(target):
        pl.semaphore_signal(barrier, inc=1, device_id=target, device_id_type=MESH)

    for dy in range(4):
        for dz in range(1, 4):
            greet({"pts": place(dy, dz, 0)})
            greet({"pts": place(dy, 8 - dz, 1)})
            greet({"pts": place(dy, (8 - dz) * (1 - half) + dz * half, half)})
        greet({"pts": place(dy, 4, 1 - half)})
        if dy:
            greet({"pts": place(dy, 0, half)})
    greet({"pts": other_core})
    greet({"pts": other_chip})
    greet({"pts": diagonal})
    greet({"grp": next_grp})
    greet({"grp": last_grp})

    loads = [
        pltpu.make_async_copy(source, target, weight_sem.at[index])
        for index, (source, target) in enumerate(
            (
                (qkv_any, qkv_ref),
                (proj_any, proj_ref),
                (up_any, up_ref),
                (down_any, down_ref),
            )
        )
    ]
    for one in loads:
        one.start()

    slot = slot_ref[...]
    owner = slot // PATCH
    position = slot % PATCH
    index = jnp.where(owner // 128 == grp, owner % 128, 0)
    quad = index // 4
    dy_of = (quad // 8 - quad_y + 4) % 4
    dz_of = (quad % 8 - quad_z + 8) % 8
    turn = dz_of - 4
    place_of = 2 * jnp.abs(turn) - (turn < 0).astype(I32)
    block_of = place_of * 4 + dy_of
    inner = jnp.where(place_of % 2 == 1, place_of + half, place_of - 1 + half)
    kord_of = jnp.where(place_of == 0, 0, jnp.where(place_of == 7, 7, inner))
    in_block = onehot(iota((32, ROWS), 0) == block_of)
    upto = onehot(iota((ROWS, ROWS), 0) <= iota((ROWS, ROWS), 1))
    counted = mm(in_block, upto)
    rank = jnp.sum(in_block.astype(F32) * counted, axis=0, keepdims=True).astype(I32) - 1
    row_of = block_of * 16 + rank
    perm = onehot(iota((ROWS, ROWS), 0) == row_of)
    rows_sorted = mm(perm, x_ref[0]).astype(BF)
    xp[...] = rows_sorted
    def columns_of(rows):
        padded = jnp.concatenate(
            [rows.astype(F32), jnp.zeros((128 - rows.shape[0], 128), F32)], axis=0
        )
        return jnp.transpose(padded).astype(I32)

    vobuf[:, :, 128:] = jnp.ones((2, PATCH, 128), BF)
    loads[0].wait()
    normed = layer_norm(rows_sorted, gain_ref[0, 0:1], shift_ref[0, 0:1])
    projected = mm(normed, qkv_ref[0]).astype(BF)
    qbuf[...] = projected[:, :WIDTH]
    kbuf[:ROWS] = projected[:, WIDTH : 2 * WIDTH]
    vobuf[0, :ROWS, :128] = projected[:, 2 * WIDTH : 2 * WIDTH + 128]
    vobuf[1, :ROWS, :128] = projected[:, 2 * WIDTH + 128 :]

    def feed_forward(rows, block):
        normed_ff = layer_norm(rows, gain_ref[block, 1:2], shift_ref[block, 1:2])
        hidden = gelu(mm(normed_ff, up_ref[block]) + upb_ref[block : block + 1]).astype(BF)
        down = mm(hidden, down_ref[block]) + outb_ref[block, 1:2]
        return (rows.astype(F32) + down).astype(BF)

    head_lane = iota((128, 128), 1) // 16

    def attend_one(rows, keys):
        totals = {}

        def score(step):
            group, pair_index = step
            queries = qbuf[rows, group * 128 : group * 128 + 128]
            masked = [
                jnp.where(head_lane == head, queries, jnp.zeros_like(queries))
                for head in (2 * pair_index, 2 * pair_index + 1)
            ]
            return mm_nt(
                jnp.concatenate(masked, axis=0), kbuf[keys, group * 128 : group * 128 + 128]
            )

        def finish(step, scores):
            group, pair_index = step
            weights = jnp.exp2(scores * SCALE).astype(BF)
            result = mm(weights, vobuf[group, keys])
            for side in range(2):
                mine = result[side * 128 : side * 128 + 128]
                head = 2 * pair_index + side
                if head == 0:
                    totals[group] = (mine[:, :128], mine[:, 128:])
                else:
                    top, bottom = totals[group]
                    totals[group] = (
                        jnp.where(head_lane == head, mine[:, :128], top),
                        jnp.where(head_lane == head, mine[:, 128:], bottom),
                    )

        pipelined([(g, h) for g in range(2) for h in range(4)], score, finish)
        return totals

    def own_keys(part, carry):
        rows = pl.ds(pl.multiple_of(part * 128, 128), 128)
        totals = attend_one(rows, slice(0, ROWS))
        for group in range(2):
            acc[rows, group * 256 : group * 256 + 128] = totals[group][0]
            acc[rows, group * 256 + 128 : group * 256 + 256] = totals[group][1]
        return carry

    lax.fori_loop(0, 2, own_keys, 0)
    pl.semaphore_wait(barrier, PEERS)
    pair = copy_to(x_ref.at[0], px, pair_sem.at[0], pair_sem.at[1], pts=other_core)
    pair.start()

    code = (index % 4) * PATCH + position
    high = in_block * (code // 64).astype(BF)
    low = in_block * (code % 64).astype(BF)
    lane_of = (kord_of % 2 * 4 + dy_of) * 16 + rank
    spread = onehot(iota((128, ROWS), 0) == lane_of)
    tags = mm_nt(high, spread) * 64.0 + mm_nt(low, spread)
    for block in range(32):
        tag_send[block] = tags[block : block + 1]

    def tag_copy(block, s, pts):
        return copy_to(tag_send.at[block], tag_recv.at[s], tag_ssem, tag_rsem, pts=pts)

    def legs(turn_index):
        first = (3 - turn_index) // 3
        last = turn_index // 3
        even = (4 + turn_index, 1 - half * first, (2 * turn_index - 1 + half) * (1 - first))
        odd = (3 - turn_index, half * last, 2 * turn_index + 1 + half * (1 - last))
        return even, odd

    for part in range(4):
        for parity, (dz, chip_half, kord) in enumerate(legs(part)):
            for dy in range(4):
                block = (2 * part + parity) * 4 + dy
                if block == 28:
                    tag_recv[28] = tag_send[28]
                else:
                    tag_copy(block, kord * 4 + dy, place(dy, dz, chip_half)).start()

    for one in loads[1:]:
        one.wait()
    pair.wait()
    normed = layer_norm(px[...], gain_ref[0, 0:1], shift_ref[0, 0:1])
    projected = mm(normed, qkv_ref[0, :, WIDTH:]).astype(BF)
    kbuf[ROWS:] = projected[:, :WIDTH]
    vobuf[0, ROWS:, :128] = projected[:, WIDTH : WIDTH + 128]
    vobuf[1, ROWS:, :128] = projected[:, WIDTH + 128 :]


    quad_copies = [
        copy_to(
            tag_quad.at[0], tag_quad.at[rel], quad_ssem.at[rel], quad_rsem.at[rel], pts=target
        )
        for rel, target in ((1, other_chip), (2, other_core), (3, diagonal))
    ]

    def share_tags():
        wait_bytes(tag_recv.at[pl.ds(0, 31)], tag_rsem)
        groups = []
        for t in range(4):
            total = tag_recv[8 * t]
            for s in range(1, 8):
                total = total + tag_recv[8 * t + s]
            groups.append(total)
        tag_quad[0] = jnp.concatenate(groups + [jnp.zeros((4, 128), F32)], axis=0)
        for one in quad_copies:
            one.start()

    def z_copy(kord):
        rows = pl.ds(kord * 64, 64)
        return copy_to(
            recv_a.at[rows], zrows.at[rows], z_ssem.at[kord], z_rsem.at[kord], pts=other_chip
        )

    def forward(kord):
        count = 48 if kord == 7 else 64
        wait_bytes(recv_a.at[pl.ds(kord * 64, count)], ab_recv.at[kord])
        z_copy(kord).start()

    def part_one(part, carry):
        rows = pl.ds(pl.multiple_of(part * 128, 128), 128)
        totals = attend_one(rows, slice(ROWS, PATCH))
        tops = [acc[rows, g * 256 : g * 256 + 128] + totals[g][0] for g in range(2)]
        bottoms = [acc[rows, g * 256 + 128 : g * 256 + 256] + totals[g][1] for g in range(2)]
        attended = jnp.concatenate(
            [(tops[g] / bottoms[g]).astype(BF) for g in range(2)], axis=1
        )
        mixed = xp[rows, :].astype(F32) + (mm(attended, proj_ref[0]) + outb_ref[0, 0:1])
        send_a[rows, :] = feed_forward(mixed.astype(BF), 0)
        for parity, (dz, chip_half, kord) in enumerate(legs(part)):
            for dy in range(4):
                block = (2 * part + parity) * 4 + dy

                def start(block=block, dz=dz, chip_half=chip_half, kord=kord, dy=dy):
                    copy_to(
                        send_a.at[pl.ds(block * 16, 16)],
                        recv_a.at[pl.ds((kord * 4 + dy) * 16, 16)],
                        ab_send,
                        ab_recv.at[kord],
                        pts=place(dy, dz, chip_half),
                    ).start()

                if parity == 1 and dy == 0:
                    pl.when(part < 3)(start)
                else:
                    start()
        pl.when(jnp.logical_or(part == 0, part == 1))(lambda: own_keys(part + 2, None))
        pl.when(part == 2)(share_tags)
        return carry

    lax.fori_loop(0, 4, part_one, 0)
    recv_a[448:464] = send_a[448:464]

    low_lane = iota((128, 128), 1) < 64
    columns = pl.multiple_of(half * 128, 128)
    mine_first = core == 0

    def project_two(rows):
        normed_two = layer_norm(rows, gain_ref[1, 0:1], shift_ref[1, 0:1])
        parts = [
            mm(normed_two, qkv_ref[1, :, pl.ds(t * WIDTH + columns, 128)]) for t in range(3)
        ]
        turned = [pltpu.roll(part, 64, 1) for part in parts]
        low = [jnp.where(mine_first, parts[t], turned[t]) for t in range(3)]
        upper = [jnp.where(mine_first, turned[t], parts[t]) for t in range(3)]
        ones = jnp.ones((128, 128), F32)
        own = [jnp.where(low_lane, low[0], upper[1]), jnp.where(low_lane, low[2], ones)]
        other = [jnp.where(low_lane, upper[0], low[1]), jnp.where(low_lane, upper[2], ones)]
        return (
            jnp.concatenate(own, axis=1).astype(BF),
            jnp.concatenate(other, axis=1).astype(BF),
        )

    def d_copy(which, part):
        rows = pl.ds(part * 128, 128)
        sem = which * 4 + part
        return copy_to(
            dsend.at[which, rows],
            gath.at[2 + which, rows],
            d_ssem.at[sem],
            d_rsem.at[sem],
            pts=other_core,
        )

    for one in quad_copies:
        one.wait_recv()
    codes = jnp.concatenate([tag_quad[rel, 0:4] for rel in range(4)], axis=0).astype(I32)
    place_in = codes // PATCH
    counts = []
    for who in range(4):
        mine = (place_in == who).astype(F32)
        mine = jnp.sum(mine, axis=1, keepdims=True)
        counts.append(jnp.sum(mine, axis=0, keepdims=True).astype(I32))
    full = [count == PATCH for count in counts]
    start_at = jnp.zeros((1, 1), I32) + PATCH
    sorted_at = codes % PATCH
    firsts = []
    for who in range(4):
        sorted_at = sorted_at + jnp.where(
            place_in == who, jnp.where(full[who], 0, start_at), 0
        )
        firsts.append(jnp.where(full[who], 0, start_at))
        start_at = start_at + jnp.where(full[who], 0, counts[who])
    zero_full = full[0]
    end_one = jnp.where(full[0], counts[1], counts[0])
    end_two = PATCH - jnp.where(full[3], counts[2], counts[3])
    cols = columns_of(sorted_at)

    def build_sort(t):
        lane_row = sorted_at[t : t + 1]

        def sort_block(block, carry):
            rows = pl.ds(pl.multiple_of(block * 256, 256), 256)
            sort_m[rows, t * 128 : t * 128 + 128] = onehot(
                iota((256, 128), 0) + block * 256 == lane_row
            )
            return carry

        lax.fori_loop(0, 8, sort_block, 0)

    for part in range(2):
        for t in range(8 * part, 8 * part + 8):
            build_sort(t)
        for kord in range(4 * part, 4 * part + 4):
            forward(kord)
    for part in range(4):
        rows = slice(part * 128, part * 128 + 128)
        gath[0, rows], dsend[0, rows] = project_two(recv_a[rows])
        d_copy(0, part).start()

    def partner_rows(part):
        rows = slice(part * 128, part * 128 + 128)
        for kord in (2 * part, 2 * part + 1):
            z_copy(kord).wait_recv()
        gath[1, rows], dsend[1, rows] = project_two(zrows[rows])
        d_copy(1, part).start()

    def sort_some(rows, rels):
        total = mm(sort_m[rows, rels[0] * 512 : rels[0] * 512 + 512], gath[rels[0]])
        for rel in rels[1:]:
            total = total + mm(sort_m[rows, rel * 512 : rel * 512 + 512], gath[rel])
        return total

    def sort_own(block, carry):
        rows = pl.ds(pl.multiple_of(block * 256, 256), 256)
        gacc[rows, :] = sort_some(rows, (0, 2))
        return carry

    for part in range(4):
        d_copy(0, part).wait_recv()
    lax.fori_loop(0, 8, sort_own, 0, unroll=2)
    for part in range(4):
        partner_rows(part)
    for part in range(4):
        d_copy(1, part).wait_recv()

    def sort_rows(block, carry):
        rows = pl.ds(pl.multiple_of(block * 256, 256), 256)
        total = gacc[rows, :] + sort_some(rows, (1, 3))
        gs[rows, :] = total.astype(BF)
        kpack[rows, :] = pltpu.roll(total[:, 0:128], 64, 1).astype(BF)
        return carry

    sort_rows(0, 0)
    sort_rows(4, 0)
    cross_out[...] = jnp.where(zero_full, gs[0:CROSS], gs[PATCH : PATCH + CROSS])
    cross = copy_to(cross_out, cross_in, cross_sem.at[0], cross_sem.at[1], group=next_grp)
    cross.start()
    for block in (1, 2, 3, 5, 6, 7):
        sort_rows(block, 0)
    for t in range(16):
        unsort_m[t * 128 : t * 128 + 128] = onehot(iota((128, 2048), 1) == cols[:, t : t + 1])
    cross.wait()
    first_quad = me < 4
    in_full = jnp.logical_and(first_quad, zero_full)
    in_rest = jnp.logical_and(first_quad, jnp.logical_not(zero_full))
    gs[0:CROSS] = jnp.where(in_full, cross_in[...], gs[0:CROSS])
    gs[PATCH : PATCH + CROSS] = jnp.where(in_rest, cross_in[...], gs[PATCH : PATCH + CROSS])
    for rows in (slice(0, CROSS), slice(PATCH, PATCH + CROSS)):
        kpack[rows] = pltpu.roll(gs[rows, 0:128].astype(F32), 64, 1).astype(BF)

    head_lane_two = iota((256, 128), 1) // 16

    def full_part(block):
        return slice(block * 256, block * 256 + 256), slice(0, PATCH), None

    def rest_part(block):
        low_key, high_key = ((0, 512), (0, 768), (256, 1024), (512, 1024))[block]
        size = high_key - low_key
        key_at = iota((1, size), 1) + low_key
        query_at = iota((256, 1), 0) + block * 256
        key_part = (key_at >= end_one).astype(I32) + (key_at >= end_two).astype(I32)
        query_part = (query_at >= end_one).astype(I32) + (query_at >= end_two).astype(I32)
        return (
            slice(PATCH + block * 256, PATCH + block * 256 + 256),
            slice(PATCH + low_key, PATCH + high_key),
            query_part == key_part,
        )

    def attend(parts):
        held = {}

        def score(step):
            query_rows, key_rows, _ = parts[step // 4]
            queries = gs[query_rows, 0:128]
            masked = jnp.where(head_lane_two == step % 4, queries, jnp.zeros_like(queries))
            return mm_nt(masked, kpack[key_rows])

        def finish(step, scores):
            query_rows, key_rows, mask = parts[step // 4]
            weights = jnp.exp2(scores * SCALE)
            if mask is not None:
                weights = jnp.where(mask, weights, 0.0)
            total = mm(weights.astype(BF), gs[key_rows, 128:256])
            if step % 4:
                total = jnp.where(head_lane_two % 4 == step % 4, total, held[step // 4])
            held[step // 4] = total
            if step % 4 == 3:
                attended = total / pltpu.roll(total, 64, 1)
                both = jnp.where(
                    iota((256, 128), 1) < 64, attended, pltpu.roll(attended, 64, 1)
                )
                att_s[query_rows] = both.astype(BF)

        pipelined(list(range(4 * len(parts))), score, finish)

    attend([full_part(0), rest_part(0)])
    catt_out[...] = jnp.where(zero_full, att_s[0:CROSS], att_s[PATCH : PATCH + CROSS])
    cross_back = copy_to(catt_out, catt_in, catt_sem.at[0], catt_sem.at[1], group=last_grp)
    cross_back.start()
    attend([full_part(1), full_part(2)])
    attend([full_part(3), rest_part(1)])
    attend([rest_part(2), rest_part(3)])
    cross_back.wait()
    att_s[0:CROSS] = jnp.where(in_full, catt_in[...], att_s[0:CROSS])
    att_s[PATCH : PATCH + CROSS] = jnp.where(
        in_rest, catt_in[...], att_s[PATCH : PATCH + CROSS]
    )

    def unsorted(rel, at, size):
        return mm(unsort_m[rel * 512 + at : rel * 512 + at + size], att_s[...])

    def att_copy(rel, part):
        rows = pl.ds(part * 128, 128)
        sem = rel * 2 + part
        return copy_to(
            att_out.at[rel, rows],
            att_in.at[rel, rows],
            at_ssem.at[sem],
            at_rsem.at[sem],
            pts=(None, other_chip, other_core, diagonal)[rel],
        )

    for part in range(2):
        rows = slice(part * 128, part * 128 + 128)
        for rel in (3, 1, 2):
            result = unsorted(rel, part * 256, 256)
            att_out[rel, rows] = jnp.where(low_lane, result[:128], result[128:]).astype(BF)
            att_copy(rel, part).start()
    for part in range(2):
        rows = slice(part * 128, part * 128 + 128)
        result = unsorted(0, part * 256, 256)
        att_in[0, rows] = jnp.where(low_lane, result[:128], result[128:]).astype(BF)

    def proj_rows(chip_half, chip_core):
        at = pl.multiple_of((chip_half * 2 + chip_core) * 64, 64)
        return proj_ref[1, pl.ds(at, 64), :]

    zeros = jnp.zeros((64, WIDTH), BF)
    owners = ((half, core), (1 - half, core), (half, 1 - core), (1 - half, 1 - core))
    for rel, (chip_half, chip_core) in enumerate(owners):
        low, high = rel * 128, rel * 128 + 64
        weights = proj_rows(chip_half, chip_core)
        wide_proj[0, low : low + 64] = weights
        wide_proj[0, high : high + 64] = zeros
        wide_proj[1, low : low + 64] = zeros
        wide_proj[1, high : high + 64] = weights

    def part_two(part, carry):
        rows = pl.ds(pl.multiple_of(part * 128, 128), 128)
        packed = pl.ds(pl.multiple_of(part // 2 * 128, 128), 128)

        def arrive():
            for rel in range(1, 4):
                att_copy(rel, part // 2).wait_recv()

        pl.when(part % 2 == 0)(arrive)
        attended = jnp.concatenate([att_in[rel, packed, :] for rel in range(4)], axis=1)
        out_rows = mm(attended, wide_proj[part % 2])
        mixed = recv_a[rows, :].astype(F32) + (out_rows + outb_ref[1, 0:1])
        ret_send[rows, :] = feed_forward(mixed.astype(BF), 1)
        first = (3 - part) // 3
        last = part // 3
        even = (4 - part + half * (2 * part), 1 - half * first, (2 * part - 1 + half) * (1 - first))
        odd = (
            3 - part + half * (2 + 2 * part),
            half * last,
            2 * part + 1 + half * (1 - last),
        )
        for parity, (dz, chip_half, place_at) in enumerate((even, odd)):
            for dy in range(4):
                s = (2 * part + parity) * 4 + dy

                def start(s=s, dz=dz, chip_half=chip_half, place_at=place_at, dy=dy):
                    copy_to(
                        ret_send.at[pl.ds(s * 16, 16)],
                        home.at[pl.ds((place_at * 4 + dy) * 16, 16)],
                        rt_ssem,
                        rt_rsem.at[place_at],
                        pts=place(-dy, -dz, chip_half),
                    ).start()

                if parity == 1 and dy == 0:
                    pl.when(part < 3)(start)
                else:
                    start()

        return carry

    lax.fori_loop(0, 4, part_two, 0)
    row_cols = columns_of(
        jnp.concatenate([row_of[:, t * 128 : t * 128 + 128] for t in range(4)], axis=0)
    )
    for t in range(4):
        home_m[t * 128 : t * 128 + 128] = onehot(iota((128, ROWS), 1) == row_cols[:, t : t + 1])
    home[448:464] = ret_send[448:464]
    for place_at in range(8):
        count = 48 if place_at == 7 else 64
        wait_bytes(home.at[pl.ds(place_at * 64, count)], rt_rsem.at[place_at])
    out_ref[0] = mm(home_m[...], home[...]).astype(BF)

    wait_bytes(tag_send.at[pl.ds(0, 31)], tag_ssem)
    for one in quad_copies:
        one.wait_send()
    wait_bytes(send_a.at[pl.ds(0, 496)], ab_send)
    for kord in range(8):
        z_copy(kord).wait_send()
    for which in range(2):
        for part in range(4):
            d_copy(which, part).wait_send()
    for rel in range(1, 4):
        for part in range(2):
            att_copy(rel, part).wait_send()
    wait_bytes(ret_send.at[pl.ds(0, 496)], rt_ssem)


def on_device(
    features,
    hilbert_slot,
    hilbert_count,
    norm_gain,
    norm_shift,
    qkv_weight,
    proj_weight,
    up_weight,
    up_bias,
    down_weight,
    out_bias,
):
    vmem = pl.BlockSpec(memory_space=pltpu.VMEM)
    sems = pltpu.SemaphoreType.DMA
    rows_buffer = pltpu.VMEM((ROWS, WIDTH), BF)
    any_space = pl.BlockSpec(memory_space=pl.ANY)
    scratch = [
        pltpu.VMEM((2, WIDTH, 3 * WIDTH), BF),
        pltpu.VMEM((2, WIDTH, WIDTH), BF),
        pltpu.VMEM((2, WIDTH, 4 * WIDTH), BF),
        pltpu.VMEM((2, 4 * WIDTH, WIDTH), BF),
        sems((4,)),
        rows_buffer,
        rows_buffer,
        pltpu.VMEM((ROWS, 2 * WIDTH), F32),
        rows_buffer,
        pltpu.VMEM((PATCH, WIDTH), BF),
        pltpu.VMEM((2, PATCH, WIDTH), BF),
        rows_buffer,
        rows_buffer,
        pltpu.VMEM((32, 1, 128), F32),
        pltpu.VMEM((32, 1, 128), F32),
        pltpu.VMEM((4, 8, 128), F32),
        rows_buffer,
        pltpu.VMEM((4, ROWS, WIDTH), BF),
        pltpu.VMEM((2, ROWS, WIDTH), BF),
        pltpu.VMEM((2 * PATCH, 2 * PATCH), BF),
        pltpu.VMEM((2 * PATCH, 2 * PATCH), BF),
        pltpu.VMEM((ROWS, ROWS), BF),
        pltpu.VMEM((2 * PATCH, WIDTH), F32),
        pltpu.VMEM((2 * PATCH, WIDTH), BF),
        pltpu.VMEM((2 * PATCH, 128), BF),
        pltpu.VMEM((CROSS, WIDTH), BF),
        pltpu.VMEM((CROSS, WIDTH), BF),
        pltpu.VMEM((2 * PATCH, 128), BF),
        pltpu.VMEM((CROSS, 128), BF),
        pltpu.VMEM((CROSS, 128), BF),
        pltpu.VMEM((4, 256, 128), BF),
        pltpu.VMEM((4, 256, 128), BF),
        pltpu.VMEM((2, 2 * WIDTH, WIDTH), BF),
        rows_buffer,
        rows_buffer,
        sems,
        sems((8,)),
        sems,
        sems,
        sems((4,)),
        sems((4,)),
        sems((2,)),
        sems((8,)),
        sems((8,)),
        sems((8,)),
        sems((8,)),
        sems((2,)),
        sems((2,)),
        sems((8,)),
        sems((8,)),
        sems,
        sems((8,)),
    ]
    return pl.pallas_call(
        kernel,
        out_shape=jax.ShapeDtypeStruct((1, ROWS, WIDTH), BF),
        in_specs=[vmem] * 4 + [any_space] * 3 + [vmem, any_space, vmem],
        out_specs=vmem,
        scratch_shapes=scratch,
        compiler_params=pltpu.CompilerParams(
            collective_id=0, has_side_effects=True, vmem_limit_bytes=60 * 2**20
        ),
    )(
        features,
        hilbert_slot,
        norm_gain,
        norm_shift,
        qkv_weight,
        proj_weight,
        up_weight,
        up_bias,
        down_weight,
        out_bias,
    )


def solution(mesh):
    return jax.shard_map(
        on_device,
        mesh=mesh,
        in_specs=(
            P("grp", "pts", None),
            P("grp", "pts"),
            P("grp", "pts"),
            P(),
            P(),
            P(),
            P(),
            P(),
            P(),
            P(),
            P(),
        ),
        out_specs=P("grp", "pts", None),
        check_vma=False,
    )
```

```python
import functools

import jax
import jax.numpy as jnp
from jax import lax
from jax.experimental import pallas as pl
from jax.experimental.pallas import tpu as pltpu
from jax.sharding import PartitionSpec as P

BF = jnp.bfloat16
F32 = jnp.float32
I32 = jnp.int32
MESH = pl.DeviceIdType.MESH
NORM_EPS = 1e-05
LOG2E = 1.4426950408889634
SCALE = 0.25 * LOG2E
ROWS = 512
WIDTH = 256
PATCH = 1024
CROSS = 64
PEERS = 48


def layer_norm(rows, gain, shift):
    rows = rows.astype(F32)
    centered = rows - jnp.mean(rows, axis=-1, keepdims=True)
    spread = jnp.mean(centered * centered, axis=-1, keepdims=True)
    return (centered * lax.rsqrt(spread + NORM_EPS) * gain + shift).astype(BF)


def mm(left, right):
    return jnp.dot(left, right, preferred_element_type=F32)


def mm_nt(left, right):
    return lax.dot_general(left, right, (((1,), (1,)), ((), ())), preferred_element_type=F32)


def iota(shape, dim):
    return lax.broadcasted_iota(I32, shape, dim)


def onehot(mask):
    return jnp.where(mask, 1.0, 0.0).astype(BF)


def gelu(values):
    size = jnp.abs(values)
    under = 1.0 + 0.23164189 * size
    t = pl.reciprocal(under, approx=True)
    t = t * (2.0 - under * t)
    poly = 0.5 * 1.061405429 * t - 0.5 * 1.453152027
    for factor in (0.5 * 1.421413741, -0.5 * 0.284496736, 0.5 * 0.254829592):
        poly = poly * t + factor
    tail = jnp.exp2(values * values * (-0.5 * LOG2E)) * (poly * t)
    return jnp.maximum(values, 0.0) - size * tail


def pipelined(parts, score, finish):
    scores = score(parts[0])
    for index, part in enumerate(parts):
        ahead = score(parts[index + 1]) if index + 1 < len(parts) else None
        finish(part, scores)
        scores = ahead


def kernel(
    x_ref,
    slot_ref,
    gain_ref,
    shift_ref,
    qkv_any,
    proj_any,
    up_any,
    upb_ref,
    down_any,
    outb_ref,
    out_ref,
    qkv_ref,
    proj_ref,
    up_ref,
    down_ref,
    weight_sem,
    px,
    xp,
    acc,
    qbuf,
    kbuf,
    vobuf,
    send_a,
    recv_a,
    tag_send,
    tag_recv,
    tag_quad,
    zrows,
    gath,
    dsend,
    sort_m,
    unsort_m,
    home_m,
    gacc,
    gs,
    kpack,
    cross_out,
    cross_in,
    att_s,
    catt_out,
    catt_in,
    att_out,
    att_in,
    wide_proj,
    ret_send,
    home,
    ab_send,
    ab_recv,
    tag_ssem,
    tag_rsem,
    quad_ssem,
    quad_rsem,
    pair_sem,
    z_ssem,
    z_rsem,
    d_ssem,
    d_rsem,
    cross_sem,
    catt_sem,
    at_ssem,
    at_rsem,
    rt_ssem,
    rt_rsem,
):
    me = lax.axis_index("pts")
    grp = lax.axis_index("grp")
    core = me % 2
    half = (me // 2) % 2
    quad_z = (me // 4) % 8
    quad_y = me // 32
    base = me // 4 * 4
    other_core = base + half * 2 + (1 - core)
    other_chip = base + (1 - half) * 2 + core
    diagonal = base + (1 - half) * 2 + (1 - core)
    next_grp = (grp + 1) % 4
    last_grp = (grp + 3) % 4

    def place(dy, dz, chip_half):
        return (((quad_y + dy + 4) % 4) * 8 + (quad_z + dz + 8) % 8) * 4 + chip_half * 2 + core

    def copy_to(src, dst, ssem, rsem, pts=None, group=None):
        target = {"pts": pts} if group is None else {"grp": group}
        return pltpu.make_async_remote_copy(
            src_ref=src,
            dst_ref=dst,
            send_sem=ssem,
            recv_sem=rsem,
            device_id=target,
            device_id_type=MESH,
        )

    def wait_bytes(view, sem):
        pltpu.make_async_copy(view, view, sem).wait()

    barrier = pltpu.get_barrier_semaphore()

    def greet(target):
        pl.semaphore_signal(barrier, inc=1, device_id=target, device_id_type=MESH)

    for dy in range(4):
        for dz in range(1, 4):
            greet({"pts": place(dy, dz, 0)})
            greet({"pts": place(dy, 8 - dz, 1)})
            greet({"pts": place(dy, (8 - dz) * (1 - half) + dz * half, half)})
        greet({"pts": place(dy, 4, 1 - half)})
        if dy:
            greet({"pts": place(dy, 0, half)})
    greet({"pts": other_core})
    greet({"pts": other_chip})
    greet({"pts": diagonal})
    greet({"grp": next_grp})
    greet({"grp": last_grp})

    loads = [
        pltpu.make_async_copy(source, target, weight_sem.at[index])
        for index, (source, target) in enumerate(
            (
                (qkv_any, qkv_ref),
                (proj_any, proj_ref),
                (up_any, up_ref),
                (down_any, down_ref),
            )
        )
    ]
    for one in loads:
        one.start()

    slot = slot_ref[...]
    owner = slot // PATCH
    position = slot % PATCH
    index = jnp.where(owner // 128 == grp, owner % 128, 0)
    quad = index // 4
    dy_of = (quad // 8 - quad_y + 4) % 4
    dz_of = (quad % 8 - quad_z + 8) % 8
    turn = dz_of - 4
    place_of = 2 * jnp.abs(turn) - (turn < 0).astype(I32)
    block_of = place_of * 4 + dy_of
    inner = jnp.where(place_of % 2 == 1, place_of + half, place_of - 1 + half)
    kord_of = jnp.where(place_of == 0, 0, jnp.where(place_of == 7, 7, inner))
    in_block = onehot(iota((32, ROWS), 0) == block_of)
    upto = onehot(iota((ROWS, ROWS), 0) <= iota((ROWS, ROWS), 1))
    counted = mm(in_block, upto)
    rank = jnp.sum(in_block.astype(F32) * counted, axis=0, keepdims=True).astype(I32) - 1
    row_of = block_of * 16 + rank
    perm = onehot(iota((ROWS, ROWS), 0) == row_of)
    rows_sorted = mm(perm, x_ref[0]).astype(BF)
    xp[...] = rows_sorted
    def columns_of(rows):
        padded = jnp.concatenate(
            [rows.astype(F32), jnp.zeros((128 - rows.shape[0], 128), F32)], axis=0
        )
        return jnp.transpose(padded).astype(I32)

    vobuf[:, :, 128:] = jnp.ones((2, PATCH, 128), BF)
    loads[0].wait()
    normed = layer_norm(rows_sorted, gain_ref[0, 0:1], shift_ref[0, 0:1])
    projected = mm(normed, qkv_ref[0]).astype(BF)
    qbuf[...] = projected[:, :WIDTH]
    kbuf[:ROWS] = projected[:, WIDTH : 2 * WIDTH]
    vobuf[0, :ROWS, :128] = projected[:, 2 * WIDTH : 2 * WIDTH + 128]
    vobuf[1, :ROWS, :128] = projected[:, 2 * WIDTH + 128 :]

    def feed_forward(rows, block):
        normed_ff = layer_norm(rows, gain_ref[block, 1:2], shift_ref[block, 1:2])
        hidden = gelu(mm(normed_ff, up_ref[block]) + upb_ref[block : block + 1]).astype(BF)
        down = mm(hidden, down_ref[block]) + outb_ref[block, 1:2]
        return (rows.astype(F32) + down).astype(BF)

    head_lane = iota((128, 128), 1) // 16

    def attend_one(rows, keys):
        totals = {}

        def score(step):
            group, pair_index = step
            queries = qbuf[rows, group * 128 : group * 128 + 128]
            masked = [
                jnp.where(head_lane == head, queries, jnp.zeros_like(queries))
                for head in (2 * pair_index, 2 * pair_index + 1)
            ]
            return mm_nt(
                jnp.concatenate(masked, axis=0), kbuf[keys, group * 128 : group * 128 + 128]
            )

        def finish(step, scores):
            group, pair_index = step
            weights = jnp.exp2(scores * SCALE).astype(BF)
            result = mm(weights, vobuf[group, keys])
            for side in range(2):
                mine = result[side * 128 : side * 128 + 128]
                head = 2 * pair_index + side
                if head == 0:
                    totals[group] = (mine[:, :128], mine[:, 128:])
                else:
                    top, bottom = totals[group]
                    totals[group] = (
                        jnp.where(head_lane == head, mine[:, :128], top),
                        jnp.where(head_lane == head, mine[:, 128:], bottom),
                    )

        pipelined([(g, h) for g in range(2) for h in range(4)], score, finish)
        return totals

    def own_keys(part, carry):
        rows = pl.ds(pl.multiple_of(part * 128, 128), 128)
        totals = attend_one(rows, slice(0, ROWS))
        for group in range(2):
            acc[rows, group * 256 : group * 256 + 128] = totals[group][0]
            acc[rows, group * 256 + 128 : group * 256 + 256] = totals[group][1]
        return carry

    lax.fori_loop(0, 3, own_keys, 0)
    pl.semaphore_wait(barrier, PEERS)
    pair = copy_to(x_ref.at[0], px, pair_sem.at[0], pair_sem.at[1], pts=other_core)
    pair.start()

    code = (index % 4) * PATCH + position
    high = in_block * (code // 64).astype(BF)
    low = in_block * (code % 64).astype(BF)
    lane_of = (kord_of % 2 * 4 + dy_of) * 16 + rank
    spread = onehot(iota((128, ROWS), 0) == lane_of)
    tags = mm_nt(high, spread) * 64.0 + mm_nt(low, spread)
    for block in range(32):
        tag_send[block] = tags[block : block + 1]

    def tag_copy(block, s, pts):
        return copy_to(tag_send.at[block], tag_recv.at[s], tag_ssem, tag_rsem, pts=pts)

    def legs(turn_index):
        first = (3 - turn_index) // 3
        last = turn_index // 3
        even = (4 + turn_index, 1 - half * first, (2 * turn_index - 1 + half) * (1 - first))
        odd = (3 - turn_index, half * last, 2 * turn_index + 1 + half * (1 - last))
        return even, odd

    for part in range(4):
        for parity, (dz, chip_half, kord) in enumerate(legs(part)):
            for dy in range(4):
                block = (2 * part + parity) * 4 + dy
                if block == 28:
                    tag_recv[28] = tag_send[28]
                else:
                    tag_copy(block, kord * 4 + dy, place(dy, dz, chip_half)).start()

    lax.fori_loop(3, 4, own_keys, 0)
    for one in loads[1:]:
        one.wait()
    pair.wait()
    normed = layer_norm(px[...], gain_ref[0, 0:1], shift_ref[0, 0:1])
    projected = mm(normed, qkv_ref[0, :, WIDTH:]).astype(BF)
    kbuf[ROWS:] = projected[:, :WIDTH]
    vobuf[0, ROWS:, :128] = projected[:, WIDTH : WIDTH + 128]
    vobuf[1, ROWS:, :128] = projected[:, WIDTH + 128 :]


    quad_copies = [
        copy_to(
            tag_quad.at[0], tag_quad.at[rel], quad_ssem.at[rel], quad_rsem.at[rel], pts=target
        )
        for rel, target in ((1, other_chip), (2, other_core), (3, diagonal))
    ]

    def share_tags():
        wait_bytes(tag_recv.at[pl.ds(0, 31)], tag_rsem)
        groups = []
        for t in range(4):
            total = tag_recv[8 * t]
            for s in range(1, 8):
                total = total + tag_recv[8 * t + s]
            groups.append(total)
        tag_quad[0] = jnp.concatenate(groups + [jnp.zeros((4, 128), F32)], axis=0)
        for one in quad_copies:
            one.start()

    def z_copy(kord):
        rows = pl.ds(kord * 64, 64)
        return copy_to(
            recv_a.at[rows], zrows.at[rows], z_ssem.at[kord], z_rsem.at[kord], pts=other_chip
        )

    def forward(kord):
        count = 48 if kord == 7 else 64
        wait_bytes(recv_a.at[pl.ds(kord * 64, count)], ab_recv.at[kord])
        z_copy(kord).start()

    def part_one(part, carry):
        rows = pl.ds(pl.multiple_of(part * 128, 128), 128)
        totals = attend_one(rows, slice(ROWS, PATCH))
        tops = [acc[rows, g * 256 : g * 256 + 128] + totals[g][0] for g in range(2)]
        bottoms = [acc[rows, g * 256 + 128 : g * 256 + 256] + totals[g][1] for g in range(2)]
        attended = jnp.concatenate(
            [(tops[g] / bottoms[g]).astype(BF) for g in range(2)], axis=1
        )
        mixed = xp[rows, :].astype(F32) + (mm(attended, proj_ref[0]) + outb_ref[0, 0:1])
        send_a[rows, :] = feed_forward(mixed.astype(BF), 0)
        for parity, (dz, chip_half, kord) in enumerate(legs(part)):
            for dy in range(4):
                block = (2 * part + parity) * 4 + dy

                def start(block=block, dz=dz, chip_half=chip_half, kord=kord, dy=dy):
                    copy_to(
                        send_a.at[pl.ds(block * 16, 16)],
                        recv_a.at[pl.ds((kord * 4 + dy) * 16, 16)],
                        ab_send,
                        ab_recv.at[kord],
                        pts=place(dy, dz, chip_half),
                    ).start()

                if parity == 1 and dy == 0:
                    pl.when(part < 3)(start)
                else:
                    start()
        pl.when(part == 2)(share_tags)
        return carry

    lax.fori_loop(0, 4, part_one, 0)
    recv_a[448:464] = send_a[448:464]

    low_lane = iota((128, 128), 1) < 64
    columns = pl.multiple_of(half * 128, 128)
    mine_first = core == 0

    def project_two(rows):
        normed_two = layer_norm(rows, gain_ref[1, 0:1], shift_ref[1, 0:1])
        parts = [
            mm(normed_two, qkv_ref[1, :, pl.ds(t * WIDTH + columns, 128)]) for t in range(3)
        ]
        turned = [pltpu.roll(part, 64, 1) for part in parts]
        low = [jnp.where(mine_first, parts[t], turned[t]) for t in range(3)]
        upper = [jnp.where(mine_first, turned[t], parts[t]) for t in range(3)]
        ones = jnp.ones((128, 128), F32)
        own = [jnp.where(low_lane, low[0], upper[1]), jnp.where(low_lane, low[2], ones)]
        other = [jnp.where(low_lane, upper[0], low[1]), jnp.where(low_lane, upper[2], ones)]
        return (
            jnp.concatenate(own, axis=1).astype(BF),
            jnp.concatenate(other, axis=1).astype(BF),
        )

    def d_copy(which, part):
        rows = pl.ds(part * 128, 128)
        sem = which * 4 + part
        return copy_to(
            dsend.at[which, rows],
            gath.at[2 + which, rows],
            d_ssem.at[sem],
            d_rsem.at[sem],
            pts=other_core,
        )

    for one in quad_copies:
        one.wait_recv()
    codes = jnp.concatenate([tag_quad[rel, 0:4] for rel in range(4)], axis=0).astype(I32)
    place_in = codes // PATCH
    counts = []
    for who in range(4):
        mine = (place_in == who).astype(F32)
        mine = jnp.sum(mine, axis=1, keepdims=True)
        counts.append(jnp.sum(mine, axis=0, keepdims=True).astype(I32))
    full = [count == PATCH for count in counts]
    start_at = jnp.zeros((1, 1), I32) + PATCH
    sorted_at = codes % PATCH
    firsts = []
    for who in range(4):
        sorted_at = sorted_at + jnp.where(
            place_in == who, jnp.where(full[who], 0, start_at), 0
        )
        firsts.append(jnp.where(full[who], 0, start_at))
        start_at = start_at + jnp.where(full[who], 0, counts[who])
    zero_full = full[0]
    end_one = jnp.where(full[0], counts[1], counts[0])
    end_two = PATCH - jnp.where(full[3], counts[2], counts[3])
    cols = columns_of(sorted_at)

    def build_sort(t):
        lane_row = sorted_at[t : t + 1]

        def sort_block(block, carry):
            rows = pl.ds(pl.multiple_of(block * 256, 256), 256)
            sort_m[rows, t * 128 : t * 128 + 128] = onehot(
                iota((256, 128), 0) + block * 256 == lane_row
            )
            return carry

        lax.fori_loop(0, 8, sort_block, 0)

    for part in range(2):
        for t in range(8 * part, 8 * part + 8):
            build_sort(t)
        for kord in range(4 * part, 4 * part + 4):
            forward(kord)
    for part in range(4):
        rows = slice(part * 128, part * 128 + 128)
        gath[0, rows], dsend[0, rows] = project_two(recv_a[rows])
        d_copy(0, part).start()

    def partner_rows(part):
        rows = slice(part * 128, part * 128 + 128)
        for kord in (2 * part, 2 * part + 1):
            z_copy(kord).wait_recv()
        gath[1, rows], dsend[1, rows] = project_two(zrows[rows])
        d_copy(1, part).start()

    def sort_some(rows, rels):
        total = mm(sort_m[rows, rels[0] * 512 : rels[0] * 512 + 512], gath[rels[0]])
        for rel in rels[1:]:
            total = total + mm(sort_m[rows, rel * 512 : rel * 512 + 512], gath[rel])
        return total

    def sort_own(block, carry):
        rows = pl.ds(pl.multiple_of(block * 256, 256), 256)
        gacc[rows, :] = sort_some(rows, (0, 2))
        return carry

    for part in range(4):
        d_copy(0, part).wait_recv()
    lax.fori_loop(0, 8, sort_own, 0, unroll=2)
    for part in range(4):
        partner_rows(part)
    for part in range(4):
        d_copy(1, part).wait_recv()

    def sort_rows(block, carry):
        rows = pl.ds(pl.multiple_of(block * 256, 256), 256)
        total = gacc[rows, :] + sort_some(rows, (1, 3))
        gs[rows, :] = total.astype(BF)
        kpack[rows, :] = pltpu.roll(total[:, 0:128], 64, 1).astype(BF)
        return carry

    sort_rows(0, 0)
    sort_rows(4, 0)
    cross_out[...] = jnp.where(zero_full, gs[0:CROSS], gs[PATCH : PATCH + CROSS])
    cross = copy_to(cross_out, cross_in, cross_sem.at[0], cross_sem.at[1], group=next_grp)
    cross.start()
    for block in (1, 2, 3, 5, 6, 7):
        sort_rows(block, 0)
    for t in range(16):
        unsort_m[t * 128 : t * 128 + 128] = onehot(iota((128, 2048), 1) == cols[:, t : t + 1])
    cross.wait()
    first_quad = me < 4
    in_full = jnp.logical_and(first_quad, zero_full)
    in_rest = jnp.logical_and(first_quad, jnp.logical_not(zero_full))
    gs[0:CROSS] = jnp.where(in_full, cross_in[...], gs[0:CROSS])
    gs[PATCH : PATCH + CROSS] = jnp.where(in_rest, cross_in[...], gs[PATCH : PATCH + CROSS])
    for rows in (slice(0, CROSS), slice(PATCH, PATCH + CROSS)):
        kpack[rows] = pltpu.roll(gs[rows, 0:128].astype(F32), 64, 1).astype(BF)

    head_lane_two = iota((256, 128), 1) // 16

    def full_part(block):
        return slice(block * 256, block * 256 + 256), slice(0, PATCH), None

    def rest_part(block):
        low_key, high_key = ((0, 512), (0, 768), (256, 1024), (512, 1024))[block]
        size = high_key - low_key
        key_at = iota((1, size), 1) + low_key
        query_at = iota((256, 1), 0) + block * 256
        key_part = (key_at >= end_one).astype(I32) + (key_at >= end_two).astype(I32)
        query_part = (query_at >= end_one).astype(I32) + (query_at >= end_two).astype(I32)
        return (
            slice(PATCH + block * 256, PATCH + block * 256 + 256),
            slice(PATCH + low_key, PATCH + high_key),
            query_part == key_part,
        )

    def attend(parts):
        held = {}

        def score(step):
            query_rows, key_rows, _ = parts[step // 4]
            queries = gs[query_rows, 0:128]
            masked = jnp.where(head_lane_two == step % 4, queries, jnp.zeros_like(queries))
            return mm_nt(masked, kpack[key_rows])

        def finish(step, scores):
            query_rows, key_rows, mask = parts[step // 4]
            weights = jnp.exp2(scores * SCALE)
            if mask is not None:
                weights = jnp.where(mask, weights, 0.0)
            total = mm(weights.astype(BF), gs[key_rows, 128:256])
            if step % 4:
                total = jnp.where(head_lane_two % 4 == step % 4, total, held[step // 4])
            held[step // 4] = total
            if step % 4 == 3:
                attended = total / pltpu.roll(total, 64, 1)
                both = jnp.where(
                    iota((256, 128), 1) < 64, attended, pltpu.roll(attended, 64, 1)
                )
                att_s[query_rows] = both.astype(BF)

        pipelined(list(range(4 * len(parts))), score, finish)

    attend([full_part(0), rest_part(0)])
    catt_out[...] = jnp.where(zero_full, att_s[0:CROSS], att_s[PATCH : PATCH + CROSS])
    cross_back = copy_to(catt_out, catt_in, catt_sem.at[0], catt_sem.at[1], group=last_grp)
    cross_back.start()
    attend([full_part(1), full_part(2)])
    attend([full_part(3), rest_part(1)])
    attend([rest_part(2), rest_part(3)])
    cross_back.wait()
    att_s[0:CROSS] = jnp.where(in_full, catt_in[...], att_s[0:CROSS])
    att_s[PATCH : PATCH + CROSS] = jnp.where(
        in_rest, catt_in[...], att_s[PATCH : PATCH + CROSS]
    )

    def unsorted(rel, at, size):
        return mm(unsort_m[rel * 512 + at : rel * 512 + at + size], att_s[...])

    def att_copy(rel, part):
        rows = pl.ds(part * 128, 128)
        sem = rel * 2 + part
        return copy_to(
            att_out.at[rel, rows],
            att_in.at[rel, rows],
            at_ssem.at[sem],
            at_rsem.at[sem],
            pts=(None, other_chip, other_core, diagonal)[rel],
        )

    for part in range(2):
        rows = slice(part * 128, part * 128 + 128)
        for rel in (3, 1, 2):
            result = unsorted(rel, part * 256, 256)
            att_out[rel, rows] = jnp.where(low_lane, result[:128], result[128:]).astype(BF)
            att_copy(rel, part).start()
    for part in range(2):
        rows = slice(part * 128, part * 128 + 128)
        result = unsorted(0, part * 256, 256)
        att_in[0, rows] = jnp.where(low_lane, result[:128], result[128:]).astype(BF)

    def proj_rows(chip_half, chip_core):
        at = pl.multiple_of((chip_half * 2 + chip_core) * 64, 64)
        return proj_ref[1, pl.ds(at, 64), :]

    zeros = jnp.zeros((64, WIDTH), BF)
    owners = ((half, core), (1 - half, core), (half, 1 - core), (1 - half, 1 - core))
    for rel, (chip_half, chip_core) in enumerate(owners):
        low, high = rel * 128, rel * 128 + 64
        weights = proj_rows(chip_half, chip_core)
        wide_proj[0, low : low + 64] = weights
        wide_proj[0, high : high + 64] = zeros
        wide_proj[1, low : low + 64] = zeros
        wide_proj[1, high : high + 64] = weights

    def part_two(part, carry):
        rows = pl.ds(pl.multiple_of(part * 128, 128), 128)
        packed = pl.ds(pl.multiple_of(part // 2 * 128, 128), 128)

        def arrive():
            for rel in range(1, 4):
                att_copy(rel, part // 2).wait_recv()

        pl.when(part % 2 == 0)(arrive)
        attended = jnp.concatenate([att_in[rel, packed, :] for rel in range(4)], axis=1)
        out_rows = mm(attended, wide_proj[part % 2])
        mixed = recv_a[rows, :].astype(F32) + (out_rows + outb_ref[1, 0:1])
        ret_send[rows, :] = feed_forward(mixed.astype(BF), 1)
        first = (3 - part) // 3
        last = part // 3
        even = (4 - part + half * (2 * part), 1 - half * first, (2 * part - 1 + half) * (1 - first))
        odd = (
            3 - part + half * (2 + 2 * part),
            half * last,
            2 * part + 1 + half * (1 - last),
        )
        for parity, (dz, chip_half, place_at) in enumerate((even, odd)):
            for dy in range(4):
                s = (2 * part + parity) * 4 + dy

                def start(s=s, dz=dz, chip_half=chip_half, place_at=place_at, dy=dy):
                    copy_to(
                        ret_send.at[pl.ds(s * 16, 16)],
                        home.at[pl.ds((place_at * 4 + dy) * 16, 16)],
                        rt_ssem,
                        rt_rsem.at[place_at],
                        pts=place(-dy, -dz, chip_half),
                    ).start()

                if parity == 1 and dy == 0:
                    pl.when(part < 3)(start)
                else:
                    start()

        return carry

    lax.fori_loop(0, 4, part_two, 0)
    row_cols = columns_of(
        jnp.concatenate([row_of[:, t * 128 : t * 128 + 128] for t in range(4)], axis=0)
    )
    for t in range(4):
        home_m[t * 128 : t * 128 + 128] = onehot(iota((128, ROWS), 1) == row_cols[:, t : t + 1])
    home[448:464] = ret_send[448:464]
    for place_at in range(8):
        count = 48 if place_at == 7 else 64
        wait_bytes(home.at[pl.ds(place_at * 64, count)], rt_rsem.at[place_at])
    out_ref[0] = mm(home_m[...], home[...]).astype(BF)

    wait_bytes(tag_send.at[pl.ds(0, 31)], tag_ssem)
    for one in quad_copies:
        one.wait_send()
    wait_bytes(send_a.at[pl.ds(0, 496)], ab_send)
    for kord in range(8):
        z_copy(kord).wait_send()
    for which in range(2):
        for part in range(4):
            d_copy(which, part).wait_send()
    for rel in range(1, 4):
        for part in range(2):
            att_copy(rel, part).wait_send()
    wait_bytes(ret_send.at[pl.ds(0, 496)], rt_ssem)


def on_device(
    features,
    hilbert_slot,
    hilbert_count,
    norm_gain,
    norm_shift,
    qkv_weight,
    proj_weight,
    up_weight,
    up_bias,
    down_weight,
    out_bias,
):
    vmem = pl.BlockSpec(memory_space=pltpu.VMEM)
    sems = pltpu.SemaphoreType.DMA
    rows_buffer = pltpu.VMEM((ROWS, WIDTH), BF)
    any_space = pl.BlockSpec(memory_space=pl.ANY)
    scratch = [
        pltpu.VMEM((2, WIDTH, 3 * WIDTH), BF),
        pltpu.VMEM((2, WIDTH, WIDTH), BF),
        pltpu.VMEM((2, WIDTH, 4 * WIDTH), BF),
        pltpu.VMEM((2, 4 * WIDTH, WIDTH), BF),
        sems((4,)),
        rows_buffer,
        rows_buffer,
        pltpu.VMEM((ROWS, 2 * WIDTH), F32),
        rows_buffer,
        pltpu.VMEM((PATCH, WIDTH), BF),
        pltpu.VMEM((2, PATCH, WIDTH), BF),
        rows_buffer,
        rows_buffer,
        pltpu.VMEM((32, 1, 128), F32),
        pltpu.VMEM((32, 1, 128), F32),
        pltpu.VMEM((4, 8, 128), F32),
        rows_buffer,
        pltpu.VMEM((4, ROWS, WIDTH), BF),
        pltpu.VMEM((2, ROWS, WIDTH), BF),
        pltpu.VMEM((2 * PATCH, 2 * PATCH), BF),
        pltpu.VMEM((2 * PATCH, 2 * PATCH), BF),
        pltpu.VMEM((ROWS, ROWS), BF),
        pltpu.VMEM((2 * PATCH, WIDTH), F32),
        pltpu.VMEM((2 * PATCH, WIDTH), BF),
        pltpu.VMEM((2 * PATCH, 128), BF),
        pltpu.VMEM((CROSS, WIDTH), BF),
        pltpu.VMEM((CROSS, WIDTH), BF),
        pltpu.VMEM((2 * PATCH, 128), BF),
        pltpu.VMEM((CROSS, 128), BF),
        pltpu.VMEM((CROSS, 128), BF),
        pltpu.VMEM((4, 256, 128), BF),
        pltpu.VMEM((4, 256, 128), BF),
        pltpu.VMEM((2, 2 * WIDTH, WIDTH), BF),
        rows_buffer,
        rows_buffer,
        sems,
        sems((8,)),
        sems,
        sems,
        sems((4,)),
        sems((4,)),
        sems((2,)),
        sems((8,)),
        sems((8,)),
        sems((8,)),
        sems((8,)),
        sems((2,)),
        sems((2,)),
        sems((8,)),
        sems((8,)),
        sems,
        sems((8,)),
    ]
    return pl.pallas_call(
        kernel,
        out_shape=jax.ShapeDtypeStruct((1, ROWS, WIDTH), BF),
        in_specs=[vmem] * 4 + [any_space] * 3 + [vmem, any_space, vmem],
        out_specs=vmem,
        scratch_shapes=scratch,
        compiler_params=pltpu.CompilerParams(
            collective_id=0, has_side_effects=True, vmem_limit_bytes=60 * 2**20
        ),
    )(
        features,
        hilbert_slot,
        norm_gain,
        norm_shift,
        qkv_weight,
        proj_weight,
        up_weight,
        up_bias,
        down_weight,
        out_bias,
    )


def solution(mesh):
    return jax.shard_map(
        on_device,
        mesh=mesh,
        in_specs=(
            P("grp", "pts", None),
            P("grp", "pts"),
            P("grp", "pts"),
            P(),
            P(),
            P(),
            P(),
            P(),
            P(),
            P(),
            P(),
        ),
        out_specs=P("grp", "pts", None),
        check_vma=False,
    )
```

```python
import functools

import jax
import jax.numpy as jnp
from jax import lax
from jax.experimental import pallas as pl
from jax.experimental.pallas import tpu as pltpu
from jax.sharding import PartitionSpec as P

BF = jnp.bfloat16
F32 = jnp.float32
I32 = jnp.int32
MESH = pl.DeviceIdType.MESH
NORM_EPS = 1e-05
LOG2E = 1.4426950408889634
SCALE = 0.25 * LOG2E
ROWS = 512
WIDTH = 256
PATCH = 1024
CROSS = 64
PEERS = 48


def layer_norm(rows, gain, shift):
    rows = rows.astype(F32)
    centered = rows - jnp.mean(rows, axis=-1, keepdims=True)
    spread = jnp.mean(centered * centered, axis=-1, keepdims=True)
    return (centered * lax.rsqrt(spread + NORM_EPS) * gain + shift).astype(BF)


def mm(left, right):
    return jnp.dot(left, right, preferred_element_type=F32)


def mm_nt(left, right):
    return lax.dot_general(left, right, (((1,), (1,)), ((), ())), preferred_element_type=F32)


def iota(shape, dim):
    return lax.broadcasted_iota(I32, shape, dim)


def onehot(mask):
    return jnp.where(mask, 1.0, 0.0).astype(BF)


def gelu(values):
    size = jnp.abs(values)
    under = 1.0 + 0.23164189 * size
    t = pl.reciprocal(under, approx=True)
    t = t * (2.0 - under * t)
    poly = 0.5 * 1.061405429 * t - 0.5 * 1.453152027
    for factor in (0.5 * 1.421413741, -0.5 * 0.284496736, 0.5 * 0.254829592):
        poly = poly * t + factor
    tail = jnp.exp2(values * values * (-0.5 * LOG2E)) * (poly * t)
    return jnp.maximum(values, 0.0) - size * tail


def pipelined(parts, score, finish):
    scores = score(parts[0])
    for index, part in enumerate(parts):
        ahead = score(parts[index + 1]) if index + 1 < len(parts) else None
        finish(part, scores)
        scores = ahead


def kernel(
    x_ref,
    slot_ref,
    gain_ref,
    shift_ref,
    qkv_any,
    proj_any,
    up_any,
    upb_ref,
    down_any,
    outb_ref,
    out_ref,
    qkv_ref,
    proj_ref,
    up_ref,
    down_ref,
    weight_sem,
    px,
    xp,
    acc,
    qbuf,
    kbuf,
    vobuf,
    send_a,
    recv_a,
    tag_send,
    tag_recv,
    tag_quad,
    zrows,
    gath,
    dsend,
    sort_m,
    unsort_m,
    home_m,
    gacc,
    gs,
    kpack,
    cross_out,
    cross_in,
    att_s,
    catt_out,
    catt_in,
    att_out,
    att_in,
    wide_proj,
    ret_send,
    home,
    ab_send,
    ab_recv,
    tag_ssem,
    tag_rsem,
    quad_ssem,
    quad_rsem,
    pair_sem,
    z_ssem,
    z_rsem,
    d_ssem,
    d_rsem,
    cross_sem,
    catt_sem,
    at_ssem,
    at_rsem,
    rt_ssem,
    rt_rsem,
):
    me = lax.axis_index("pts")
    grp = lax.axis_index("grp")
    core = me % 2
    half = (me // 2) % 2
    quad_z = (me // 4) % 8
    quad_y = me // 32
    base = me // 4 * 4
    other_core = base + half * 2 + (1 - core)
    other_chip = base + (1 - half) * 2 + core
    diagonal = base + (1 - half) * 2 + (1 - core)
    next_grp = (grp + 1) % 4
    last_grp = (grp + 3) % 4

    def place(dy, dz, chip_half):
        return (((quad_y + dy + 4) % 4) * 8 + (quad_z + dz + 8) % 8) * 4 + chip_half * 2 + core

    def copy_to(src, dst, ssem, rsem, pts=None, group=None):
        target = {"pts": pts} if group is None else {"grp": group}
        return pltpu.make_async_remote_copy(
            src_ref=src,
            dst_ref=dst,
            send_sem=ssem,
            recv_sem=rsem,
            device_id=target,
            device_id_type=MESH,
        )

    def wait_bytes(view, sem):
        pltpu.make_async_copy(view, view, sem).wait()

    barrier = pltpu.get_barrier_semaphore()

    def greet(target):
        pl.semaphore_signal(barrier, inc=1, device_id=target, device_id_type=MESH)

    for dy in range(4):
        for dz in range(1, 4):
            greet({"pts": place(dy, dz, 0)})
            greet({"pts": place(dy, 8 - dz, 1)})
            greet({"pts": place(dy, (8 - dz) * (1 - half) + dz * half, half)})
        greet({"pts": place(dy, 4, 1 - half)})
        if dy:
            greet({"pts": place(dy, 0, half)})
    greet({"pts": other_core})
    greet({"pts": other_chip})
    greet({"pts": diagonal})
    greet({"grp": next_grp})
    greet({"grp": last_grp})

    loads = [
        pltpu.make_async_copy(source, target, weight_sem.at[index])
        for index, (source, target) in enumerate(
            (
                (qkv_any, qkv_ref),
                (proj_any, proj_ref),
                (up_any, up_ref),
                (down_any, down_ref),
            )
        )
    ]
    for one in loads:
        one.start()

    slot = slot_ref[...]
    owner = slot // PATCH
    position = slot % PATCH
    index = jnp.where(owner // 128 == grp, owner % 128, 0)
    quad = index // 4
    dy_of = (quad // 8 - quad_y + 4) % 4
    dz_of = (quad % 8 - quad_z + 8) % 8
    turn = dz_of - 4
    place_of = 2 * jnp.abs(turn) - (turn < 0).astype(I32)
    block_of = place_of * 4 + dy_of
    inner = jnp.where(place_of % 2 == 1, place_of + half, place_of - 1 + half)
    kord_of = jnp.where(place_of == 0, 0, jnp.where(place_of == 7, 7, inner))
    in_block = onehot(iota((32, ROWS), 0) == block_of)
    upto = onehot(iota((ROWS, ROWS), 0) <= iota((ROWS, ROWS), 1))
    counted = mm(in_block, upto)
    rank = jnp.sum(in_block.astype(F32) * counted, axis=0, keepdims=True).astype(I32) - 1
    row_of = block_of * 16 + rank
    perm = onehot(iota((ROWS, ROWS), 0) == row_of)
    rows_sorted = mm(perm, x_ref[0]).astype(BF)
    xp[...] = rows_sorted
    def columns_of(rows):
        padded = jnp.concatenate(
            [rows.astype(F32), jnp.zeros((128 - rows.shape[0], 128), F32)], axis=0
        )
        return jnp.transpose(padded).astype(I32)

    vobuf[:, :, 128:] = jnp.ones((2, PATCH, 128), BF)
    loads[0].wait()
    normed = layer_norm(rows_sorted, gain_ref[0, 0:1], shift_ref[0, 0:1])
    projected = mm(normed, qkv_ref[0]).astype(BF)
    qbuf[...] = projected[:, :WIDTH]
    kbuf[:ROWS] = projected[:, WIDTH : 2 * WIDTH]
    vobuf[0, :ROWS, :128] = projected[:, 2 * WIDTH : 2 * WIDTH + 128]
    vobuf[1, :ROWS, :128] = projected[:, 2 * WIDTH + 128 :]

    def feed_forward(rows, block):
        normed_ff = layer_norm(rows, gain_ref[block, 1:2], shift_ref[block, 1:2])
        hidden = gelu(mm(normed_ff, up_ref[block]) + upb_ref[block : block + 1]).astype(BF)
        down = mm(hidden, down_ref[block]) + outb_ref[block, 1:2]
        return (rows.astype(F32) + down).astype(BF)

    head_lane = iota((128, 128), 1) // 16

    def attend_one(rows, keys):
        totals = {}

        def score(step):
            group, pair_index = step
            queries = qbuf[rows, group * 128 : group * 128 + 128]
            masked = [
                jnp.where(head_lane == head, queries, jnp.zeros_like(queries))
                for head in (2 * pair_index, 2 * pair_index + 1)
            ]
            return mm_nt(
                jnp.concatenate(masked, axis=0), kbuf[keys, group * 128 : group * 128 + 128]
            )

        def finish(step, scores):
            group, pair_index = step
            weights = jnp.exp2(scores * SCALE).astype(BF)
            result = mm(weights, vobuf[group, keys])
            for side in range(2):
                mine = result[side * 128 : side * 128 + 128]
                head = 2 * pair_index + side
                if head == 0:
                    totals[group] = (mine[:, :128], mine[:, 128:])
                else:
                    top, bottom = totals[group]
                    totals[group] = (
                        jnp.where(head_lane == head, mine[:, :128], top),
                        jnp.where(head_lane == head, mine[:, 128:], bottom),
                    )

        pipelined([(g, h) for g in range(2) for h in range(4)], score, finish)
        return totals

    def own_keys(part, carry):
        rows = pl.ds(pl.multiple_of(part * 128, 128), 128)
        totals = attend_one(rows, slice(0, ROWS))
        for group in range(2):
            acc[rows, group * 256 : group * 256 + 128] = totals[group][0]
            acc[rows, group * 256 + 128 : group * 256 + 256] = totals[group][1]
        return carry

    lax.fori_loop(0, 3, own_keys, 0)
    pl.semaphore_wait(barrier, PEERS)
    pair = copy_to(x_ref.at[0], px, pair_sem.at[0], pair_sem.at[1], pts=other_core)
    pair.start()

    code = (index % 4) * PATCH + position
    high = in_block * (code // 64).astype(BF)
    low = in_block * (code % 64).astype(BF)
    lane_of = (kord_of % 2 * 4 + dy_of) * 16 + rank
    spread = onehot(iota((128, ROWS), 0) == lane_of)
    tags = mm_nt(high, spread) * 64.0 + mm_nt(low, spread)
    for block in range(32):
        tag_send[block] = tags[block : block + 1]

    def tag_copy(block, s, pts):
        return copy_to(tag_send.at[block], tag_recv.at[s], tag_ssem, tag_rsem, pts=pts)

    def legs(turn_index):
        first = (3 - turn_index) // 3
        last = turn_index // 3
        even = (4 + turn_index, 1 - half * first, (2 * turn_index - 1 + half) * (1 - first))
        odd = (3 - turn_index, half * last, 2 * turn_index + 1 + half * (1 - last))
        return even, odd

    for part in range(4):
        for parity, (dz, chip_half, kord) in enumerate(legs(part)):
            for dy in range(4):
                block = (2 * part + parity) * 4 + dy
                if block == 28:
                    tag_recv[28] = tag_send[28]
                else:
                    tag_copy(block, kord * 4 + dy, place(dy, dz, chip_half)).start()

    lax.fori_loop(3, 4, own_keys, 0)
    for one in loads[1:]:
        one.wait()
    pair.wait()
    normed = layer_norm(px[...], gain_ref[0, 0:1], shift_ref[0, 0:1])
    projected = mm(normed, qkv_ref[0, :, WIDTH:]).astype(BF)
    kbuf[ROWS:] = projected[:, :WIDTH]
    vobuf[0, ROWS:, :128] = projected[:, WIDTH : WIDTH + 128]
    vobuf[1, ROWS:, :128] = projected[:, WIDTH + 128 :]


    quad_copies = [
        copy_to(
            tag_quad.at[0], tag_quad.at[rel], quad_ssem.at[rel], quad_rsem.at[rel], pts=target
        )
        for rel, target in ((1, other_chip), (2, other_core), (3, diagonal))
    ]

    def share_tags():
        wait_bytes(tag_recv.at[pl.ds(0, 31)], tag_rsem)
        groups = []
        for t in range(4):
            total = tag_recv[8 * t]
            for s in range(1, 8):
                total = total + tag_recv[8 * t + s]
            groups.append(total)
        tag_quad[0] = jnp.concatenate(groups + [jnp.zeros((4, 128), F32)], axis=0)
        for one in quad_copies:
            one.start()

    def z_copy(kord):
        rows = pl.ds(kord * 64, 64)
        return copy_to(
            recv_a.at[rows], zrows.at[rows], z_ssem.at[kord], z_rsem.at[kord], pts=other_chip
        )

    def forward(kord):
        count = 48 if kord == 7 else 64
        wait_bytes(recv_a.at[pl.ds(kord * 64, count)], ab_recv.at[kord])
        z_copy(kord).start()

    def part_one(part, carry):
        rows = pl.ds(pl.multiple_of(part * 128, 128), 128)
        totals = attend_one(rows, slice(ROWS, PATCH))
        tops = [acc[rows, g * 256 : g * 256 + 128] + totals[g][0] for g in range(2)]
        bottoms = [acc[rows, g * 256 + 128 : g * 256 + 256] + totals[g][1] for g in range(2)]
        attended = jnp.concatenate(
            [(tops[g] / bottoms[g]).astype(BF) for g in range(2)], axis=1
        )
        mixed = xp[rows, :].astype(F32) + (mm(attended, proj_ref[0]) + outb_ref[0, 0:1])
        send_a[rows, :] = feed_forward(mixed.astype(BF), 0)
        for parity, (dz, chip_half, kord) in enumerate(legs(part)):
            for dy in range(4):
                block = (2 * part + parity) * 4 + dy

                def start(block=block, dz=dz, chip_half=chip_half, kord=kord, dy=dy):
                    copy_to(
                        send_a.at[pl.ds(block * 16, 16)],
                        recv_a.at[pl.ds((kord * 4 + dy) * 16, 16)],
                        ab_send,
                        ab_recv.at[kord],
                        pts=place(dy, dz, chip_half),
                    ).start()

                if parity == 1 and dy == 0:
                    pl.when(part < 3)(start)
                else:
                    start()
        pl.when(part == 1)(share_tags)
        return carry

    lax.fori_loop(0, 4, part_one, 0)
    recv_a[448:464] = send_a[448:464]

    low_lane = iota((128, 128), 1) < 64
    columns = pl.multiple_of(half * 128, 128)
    mine_first = core == 0

    def project_two(rows):
        normed_two = layer_norm(rows, gain_ref[1, 0:1], shift_ref[1, 0:1])
        parts = [
            mm(normed_two, qkv_ref[1, :, pl.ds(t * WIDTH + columns, 128)]) for t in range(3)
        ]
        turned = [pltpu.roll(part, 64, 1) for part in parts]
        low = [jnp.where(mine_first, parts[t], turned[t]) for t in range(3)]
        upper = [jnp.where(mine_first, turned[t], parts[t]) for t in range(3)]
        ones = jnp.ones((128, 128), F32)
        own = [jnp.where(low_lane, low[0], upper[1]), jnp.where(low_lane, low[2], ones)]
        other = [jnp.where(low_lane, upper[0], low[1]), jnp.where(low_lane, upper[2], ones)]
        return (
            jnp.concatenate(own, axis=1).astype(BF),
            jnp.concatenate(other, axis=1).astype(BF),
        )

    def d_copy(which, part):
        rows = pl.ds(part * 128, 128)
        sem = which * 4 + part
        return copy_to(
            dsend.at[which, rows],
            gath.at[2 + which, rows],
            d_ssem.at[sem],
            d_rsem.at[sem],
            pts=other_core,
        )

    for one in quad_copies:
        one.wait_recv()
    codes = jnp.concatenate([tag_quad[rel, 0:4] for rel in range(4)], axis=0).astype(I32)
    place_in = codes // PATCH
    counts = []
    for who in range(4):
        mine = (place_in == who).astype(F32)
        mine = jnp.sum(mine, axis=1, keepdims=True)
        counts.append(jnp.sum(mine, axis=0, keepdims=True).astype(I32))
    full = [count == PATCH for count in counts]
    start_at = jnp.zeros((1, 1), I32) + PATCH
    sorted_at = codes % PATCH
    firsts = []
    for who in range(4):
        sorted_at = sorted_at + jnp.where(
            place_in == who, jnp.where(full[who], 0, start_at), 0
        )
        firsts.append(jnp.where(full[who], 0, start_at))
        start_at = start_at + jnp.where(full[who], 0, counts[who])
    zero_full = full[0]
    end_one = jnp.where(full[0], counts[1], counts[0])
    end_two = PATCH - jnp.where(full[3], counts[2], counts[3])
    cols = columns_of(sorted_at)

    def build_sort(t):
        lane_row = sorted_at[t : t + 1]

        def sort_block(block, carry):
            rows = pl.ds(pl.multiple_of(block * 256, 256), 256)
            sort_m[rows, t * 128 : t * 128 + 128] = onehot(
                iota((256, 128), 0) + block * 256 == lane_row
            )
            return carry

        lax.fori_loop(0, 8, sort_block, 0)

    for part in range(2):
        for t in range(8 * part, 8 * part + 8):
            build_sort(t)
        for kord in range(4 * part, 4 * part + 4):
            forward(kord)
    for part in range(4):
        rows = slice(part * 128, part * 128 + 128)
        gath[0, rows], dsend[0, rows] = project_two(recv_a[rows])
        d_copy(0, part).start()

    def partner_rows(part):
        rows = slice(part * 128, part * 128 + 128)
        for kord in (2 * part, 2 * part + 1):
            z_copy(kord).wait_recv()
        gath[1, rows], dsend[1, rows] = project_two(zrows[rows])
        d_copy(1, part).start()

    def sort_some(rows, rels):
        total = mm(sort_m[rows, rels[0] * 512 : rels[0] * 512 + 512], gath[rels[0]])
        for rel in rels[1:]:
            total = total + mm(sort_m[rows, rel * 512 : rel * 512 + 512], gath[rel])
        return total

    def sort_own(block, carry):
        rows = pl.ds(pl.multiple_of(block * 256, 256), 256)
        gacc[rows, :] = sort_some(rows, (0, 2))
        return carry

    for part in range(4):
        d_copy(0, part).wait_recv()
    lax.fori_loop(0, 8, sort_own, 0, unroll=2)
    for part in range(4):
        partner_rows(part)
    for part in range(4):
        d_copy(1, part).wait_recv()

    def sort_rows(block, carry):
        rows = pl.ds(pl.multiple_of(block * 256, 256), 256)
        total = gacc[rows, :] + sort_some(rows, (1, 3))
        gs[rows, :] = total.astype(BF)
        kpack[rows, :] = pltpu.roll(total[:, 0:128], 64, 1).astype(BF)
        return carry

    sort_rows(0, 0)
    sort_rows(4, 0)
    cross_out[...] = jnp.where(zero_full, gs[0:CROSS], gs[PATCH : PATCH + CROSS])
    cross = copy_to(cross_out, cross_in, cross_sem.at[0], cross_sem.at[1], group=next_grp)
    cross.start()
    for block in (1, 2, 3, 5, 6, 7):
        sort_rows(block, 0)
    for t in range(16):
        unsort_m[t * 128 : t * 128 + 128] = onehot(iota((128, 2048), 1) == cols[:, t : t + 1])
    cross.wait()
    first_quad = me < 4
    in_full = jnp.logical_and(first_quad, zero_full)
    in_rest = jnp.logical_and(first_quad, jnp.logical_not(zero_full))
    gs[0:CROSS] = jnp.where(in_full, cross_in[...], gs[0:CROSS])
    gs[PATCH : PATCH + CROSS] = jnp.where(in_rest, cross_in[...], gs[PATCH : PATCH + CROSS])
    for rows in (slice(0, CROSS), slice(PATCH, PATCH + CROSS)):
        kpack[rows] = pltpu.roll(gs[rows, 0:128].astype(F32), 64, 1).astype(BF)

    head_lane_two = iota((256, 128), 1) // 16

    def full_part(block):
        return slice(block * 256, block * 256 + 256), slice(0, PATCH), None

    def rest_part(block):
        low_key, high_key = ((0, 512), (0, 768), (256, 1024), (512, 1024))[block]
        size = high_key - low_key
        key_at = iota((1, size), 1) + low_key
        query_at = iota((256, 1), 0) + block * 256
        key_part = (key_at >= end_one).astype(I32) + (key_at >= end_two).astype(I32)
        query_part = (query_at >= end_one).astype(I32) + (query_at >= end_two).astype(I32)
        return (
            slice(PATCH + block * 256, PATCH + block * 256 + 256),
            slice(PATCH + low_key, PATCH + high_key),
            query_part == key_part,
        )

    def attend(parts):
        held = {}

        def score(step):
            query_rows, key_rows, _ = parts[step // 4]
            queries = gs[query_rows, 0:128]
            masked = jnp.where(head_lane_two == step % 4, queries, jnp.zeros_like(queries))
            return mm_nt(masked, kpack[key_rows])

        def finish(step, scores):
            query_rows, key_rows, mask = parts[step // 4]
            weights = jnp.exp2(scores * SCALE)
            if mask is not None:
                weights = jnp.where(mask, weights, 0.0)
            total = mm(weights.astype(BF), gs[key_rows, 128:256])
            if step % 4:
                total = jnp.where(head_lane_two % 4 == step % 4, total, held[step // 4])
            held[step // 4] = total
            if step % 4 == 3:
                attended = total / pltpu.roll(total, 64, 1)
                both = jnp.where(
                    iota((256, 128), 1) < 64, attended, pltpu.roll(attended, 64, 1)
                )
                att_s[query_rows] = both.astype(BF)

        pipelined(list(range(4 * len(parts))), score, finish)

    attend([full_part(0), rest_part(0)])
    catt_out[...] = jnp.where(zero_full, att_s[0:CROSS], att_s[PATCH : PATCH + CROSS])
    cross_back = copy_to(catt_out, catt_in, catt_sem.at[0], catt_sem.at[1], group=last_grp)
    cross_back.start()
    attend([full_part(1), full_part(2)])
    attend([full_part(3), rest_part(1)])
    attend([rest_part(2), rest_part(3)])
    cross_back.wait()
    att_s[0:CROSS] = jnp.where(in_full, catt_in[...], att_s[0:CROSS])
    att_s[PATCH : PATCH + CROSS] = jnp.where(
        in_rest, catt_in[...], att_s[PATCH : PATCH + CROSS]
    )

    def unsorted(rel, at, size):
        return mm(unsort_m[rel * 512 + at : rel * 512 + at + size], att_s[...])

    def att_copy(rel, part):
        rows = pl.ds(part * 128, 128)
        sem = rel * 2 + part
        return copy_to(
            att_out.at[rel, rows],
            att_in.at[rel, rows],
            at_ssem.at[sem],
            at_rsem.at[sem],
            pts=(None, other_chip, other_core, diagonal)[rel],
        )

    for part in range(2):
        rows = slice(part * 128, part * 128 + 128)
        for rel in (3, 1, 2):
            result = unsorted(rel, part * 256, 256)
            att_out[rel, rows] = jnp.where(low_lane, result[:128], result[128:]).astype(BF)
            att_copy(rel, part).start()
    for part in range(2):
        rows = slice(part * 128, part * 128 + 128)
        result = unsorted(0, part * 256, 256)
        att_in[0, rows] = jnp.where(low_lane, result[:128], result[128:]).astype(BF)

    def proj_rows(chip_half, chip_core):
        at = pl.multiple_of((chip_half * 2 + chip_core) * 64, 64)
        return proj_ref[1, pl.ds(at, 64), :]

    zeros = jnp.zeros((64, WIDTH), BF)
    owners = ((half, core), (1 - half, core), (half, 1 - core), (1 - half, 1 - core))
    for rel, (chip_half, chip_core) in enumerate(owners):
        low, high = rel * 128, rel * 128 + 64
        weights = proj_rows(chip_half, chip_core)
        wide_proj[0, low : low + 64] = weights
        wide_proj[0, high : high + 64] = zeros
        wide_proj[1, low : low + 64] = zeros
        wide_proj[1, high : high + 64] = weights

    def part_two(part, carry):
        rows = pl.ds(pl.multiple_of(part * 128, 128), 128)
        packed = pl.ds(pl.multiple_of(part // 2 * 128, 128), 128)

        def arrive():
            for rel in range(1, 4):
                att_copy(rel, part // 2).wait_recv()

        pl.when(part % 2 == 0)(arrive)
        attended = jnp.concatenate([att_in[rel, packed, :] for rel in range(4)], axis=1)
        out_rows = mm(attended, wide_proj[part % 2])
        mixed = recv_a[rows, :].astype(F32) + (out_rows + outb_ref[1, 0:1])
        ret_send[rows, :] = feed_forward(mixed.astype(BF), 1)
        first = (3 - part) // 3
        last = part // 3
        even = (4 - part + half * (2 * part), 1 - half * first, (2 * part - 1 + half) * (1 - first))
        odd = (
            3 - part + half * (2 + 2 * part),
            half * last,
            2 * part + 1 + half * (1 - last),
        )
        for parity, (dz, chip_half, place_at) in enumerate((even, odd)):
            for dy in range(4):
                s = (2 * part + parity) * 4 + dy

                def start(s=s, dz=dz, chip_half=chip_half, place_at=place_at, dy=dy):
                    copy_to(
                        ret_send.at[pl.ds(s * 16, 16)],
                        home.at[pl.ds((place_at * 4 + dy) * 16, 16)],
                        rt_ssem,
                        rt_rsem.at[place_at],
                        pts=place(-dy, -dz, chip_half),
                    ).start()

                if parity == 1 and dy == 0:
                    pl.when(part < 3)(start)
                else:
                    start()

        return carry

    lax.fori_loop(0, 4, part_two, 0)
    row_cols = columns_of(
        jnp.concatenate([row_of[:, t * 128 : t * 128 + 128] for t in range(4)], axis=0)
    )
    for t in range(4):
        home_m[t * 128 : t * 128 + 128] = onehot(iota((128, ROWS), 1) == row_cols[:, t : t + 1])
    home[448:464] = ret_send[448:464]
    for place_at in range(8):
        count = 48 if place_at == 7 else 64
        wait_bytes(home.at[pl.ds(place_at * 64, count)], rt_rsem.at[place_at])
    out_ref[0] = mm(home_m[...], home[...]).astype(BF)

    wait_bytes(tag_send.at[pl.ds(0, 31)], tag_ssem)
    for one in quad_copies:
        one.wait_send()
    wait_bytes(send_a.at[pl.ds(0, 496)], ab_send)
    for kord in range(8):
        z_copy(kord).wait_send()
    for which in range(2):
        for part in range(4):
            d_copy(which, part).wait_send()
    for rel in range(1, 4):
        for part in range(2):
            att_copy(rel, part).wait_send()
    wait_bytes(ret_send.at[pl.ds(0, 496)], rt_ssem)


def on_device(
    features,
    hilbert_slot,
    hilbert_count,
    norm_gain,
    norm_shift,
    qkv_weight,
    proj_weight,
    up_weight,
    up_bias,
    down_weight,
    out_bias,
):
    vmem = pl.BlockSpec(memory_space=pltpu.VMEM)
    sems = pltpu.SemaphoreType.DMA
    rows_buffer = pltpu.VMEM((ROWS, WIDTH), BF)
    any_space = pl.BlockSpec(memory_space=pl.ANY)
    scratch = [
        pltpu.VMEM((2, WIDTH, 3 * WIDTH), BF),
        pltpu.VMEM((2, WIDTH, WIDTH), BF),
        pltpu.VMEM((2, WIDTH, 4 * WIDTH), BF),
        pltpu.VMEM((2, 4 * WIDTH, WIDTH), BF),
        sems((4,)),
        rows_buffer,
        rows_buffer,
        pltpu.VMEM((ROWS, 2 * WIDTH), F32),
        rows_buffer,
        pltpu.VMEM((PATCH, WIDTH), BF),
        pltpu.VMEM((2, PATCH, WIDTH), BF),
        rows_buffer,
        rows_buffer,
        pltpu.VMEM((32, 1, 128), F32),
        pltpu.VMEM((32, 1, 128), F32),
        pltpu.VMEM((4, 8, 128), F32),
        rows_buffer,
        pltpu.VMEM((4, ROWS, WIDTH), BF),
        pltpu.VMEM((2, ROWS, WIDTH), BF),
        pltpu.VMEM((2 * PATCH, 2 * PATCH), BF),
        pltpu.VMEM((2 * PATCH, 2 * PATCH), BF),
        pltpu.VMEM((ROWS, ROWS), BF),
        pltpu.VMEM((2 * PATCH, WIDTH), F32),
        pltpu.VMEM((2 * PATCH, WIDTH), BF),
        pltpu.VMEM((2 * PATCH, 128), BF),
        pltpu.VMEM((CROSS, WIDTH), BF),
        pltpu.VMEM((CROSS, WIDTH), BF),
        pltpu.VMEM((2 * PATCH, 128), BF),
        pltpu.VMEM((CROSS, 128), BF),
        pltpu.VMEM((CROSS, 128), BF),
        pltpu.VMEM((4, 256, 128), BF),
        pltpu.VMEM((4, 256, 128), BF),
        pltpu.VMEM((2, 2 * WIDTH, WIDTH), BF),
        rows_buffer,
        rows_buffer,
        sems,
        sems((8,)),
        sems,
        sems,
        sems((4,)),
        sems((4,)),
        sems((2,)),
        sems((8,)),
        sems((8,)),
        sems((8,)),
        sems((8,)),
        sems((2,)),
        sems((2,)),
        sems((8,)),
        sems((8,)),
        sems,
        sems((8,)),
    ]
    return pl.pallas_call(
        kernel,
        out_shape=jax.ShapeDtypeStruct((1, ROWS, WIDTH), BF),
        in_specs=[vmem] * 4 + [any_space] * 3 + [vmem, any_space, vmem],
        out_specs=vmem,
        scratch_shapes=scratch,
        compiler_params=pltpu.CompilerParams(
            collective_id=0, has_side_effects=True, vmem_limit_bytes=60 * 2**20
        ),
    )(
        features,
        hilbert_slot,
        norm_gain,
        norm_shift,
        qkv_weight,
        proj_weight,
        up_weight,
        up_bias,
        down_weight,
        out_bias,
    )


def solution(mesh):
    return jax.shard_map(
        on_device,
        mesh=mesh,
        in_specs=(
            P("grp", "pts", None),
            P("grp", "pts"),
            P("grp", "pts"),
            P(),
            P(),
            P(),
            P(),
            P(),
            P(),
            P(),
            P(),
        ),
        out_specs=P("grp", "pts", None),
        check_vma=False,
    )
```
